256 devices in a mesh: expert: 64 (over y, z, core), etp: 4 (over x).
Axes of the slice: x: 4, y: 4, z: 8, core: 2. Of those that a mesh axis runs over, the one named last changes fastest.
Arguments:
- tokens: bfloat16 [8192, 1536], P('expert', 'etp'), may hold values from -6 to 6
- out_grad: bfloat16 [8192, 1536], P('expert', 'etp'), may hold values from -6 to 6
- expert_ids: int32 [8192, 4], P('expert'), may hold values from 0 to 63, as said below
- combine: bfloat16 [8192, 4], P('expert'), may hold values from 0.049804688 to 1
- w_gate: bfloat16 [64, 1536, 1536], P('expert', None, 'etp'), may hold values from -0.15625 to 0.15625
- w_up: bfloat16 [64, 1536, 1536], P('expert', None, 'etp'), may hold values from -0.15625 to 0.15625
- w_down: bfloat16 [64, 1536, 1536], P('expert', 'etp'), may hold values from -0.15625 to 0.15625
Outputs:
- grad_tokens: bfloat16 [8192, 1536], P('expert', 'etp')
- grad_combine: float32 [8192, 4], P('expert')
- grad_gate: float32 [64, 1536, 1536], P('expert', None, 'etp')
- grad_up: float32 [64, 1536, 1536], P('expert', None, 'etp')
- grad_down: float32 [64, 1536, 1536], P('expert', 'etp')
The draws below stay inside these ranges and needn't reach their ends.
Inputs may be any that keep to these rules, and one draw needn't show every extreme that they name: `expert_ids`: each row names 4 different experts. In each aligned block of 128 rows no expert is named by more than 16 rows, and one expert, the same in every block, is named by exactly 16 rows of every block.
All inputs are finite; a program needn't handle non-finite values.
Results may differ from the reference program's by a relative error of at most 0.007.
Values may be sent and summed in bfloat16 or wider, within the bound.
A program may use at most 128 MiB of HBM per device.

```python
import math
import jax
import jax.numpy as jnp
from jax import lax

D = 1536
FF = 1536
TOP = 4
TOK_DEV = 128
TOKENS = 8192
EXPERTS = 64
CAP = 16


def draw_expert_ids(key, part):
    key = jax.random.fold_in(key, 11)
    block_count = TOKENS // TOK_DEV
    half_cap = CAP // 2
    hot_expert = jax.random.randint(jax.random.fold_in(key, 1), (), 0, EXPERTS).astype(jnp.int32)

    def one_block(block_key):
        shuffled = jax.random.permutation(jax.random.fold_in(block_key, 1), EXPERTS).astype(jnp.int32)
        hot_place = jnp.argmax((shuffled == hot_expert).astype(jnp.int32))
        front = shuffled[0]
        shuffled = shuffled.at[hot_place].set(front).at[0].set(hot_expert)
        shifts = jax.random.randint(jax.random.fold_in(block_key, 2), (EXPERTS // 2,), 0, half_cap + 1).astype(jnp.int32)
        shifts = shifts.at[0].set(half_cap)
        expert_loads = jnp.full((EXPERTS,), half_cap, jnp.int32)
        expert_loads = expert_loads.at[shuffled[0::2]].add(shifts).at[shuffled[1::2]].add(-shifts)
        load_ends = jnp.cumsum(expert_loads).astype(jnp.int32)
        positions = jnp.arange(TOK_DEV * TOP, dtype=jnp.int32)
        labels = jnp.sum((load_ends[None, :] <= positions[:, None]).astype(jnp.int32), axis=1)
        id_table = labels.reshape(TOP, TOK_DEV).T
        row_order = jax.random.permutation(jax.random.fold_in(block_key, 3), TOK_DEV)
        return id_table[row_order]
    block_keys = jax.random.split(jax.random.fold_in(key, 2), block_count)
    drawn = jax.vmap(one_block)(block_keys)
    return drawn.reshape(TOKENS, TOP).astype(jnp.int32)


def level_of(stream_key, shape, cuts, least, largest):
    def one(position, shards_of):
        draws = jax.random.uniform(jax.random.fold_in(jax.random.fold_in(stream_key, 6), position), (shards_of,), jnp.float32, least / len(cuts), largest / len(cuts))
        return jnp.repeat(jnp.exp(draws), shape[position] // shards_of).reshape((-1,) + (1,) * (len(shape) - position - 1))

    gain = one(*cuts[0])
    for cut in cuts[1:]:
        gain = gain * one(*cut)
    return gain


def centred(own_key, dims, scale, most, shards=(), held_as=jnp.bfloat16):
    entries = scale * jax.random.normal(own_key, dims, jnp.float32)
    if shards:
        entries = entries * level_of(own_key, dims, shards, -0.22, 0.18)
    return jnp.clip(entries, -most, most).astype(held_as)


def setup_inputs(seed: int = 0) -> dict:
    arg_keys = jax.random.split(jax.random.key(seed), 8)
    tokens = centred(arg_keys[0], (TOKENS, D), 1.0, 6.0, ((0, 64), (1, 4)))
    out_grad = centred(arg_keys[1], (TOKENS, D), 1.0, 6.0, ((0, 64), (1, 4)))
    expert_ids = draw_expert_ids(jax.random.fold_in(arg_keys[7], 71), 0)
    combine = jnp.clip(jnp.exp(math.log(1.0) - 2.9996462 * jax.random.uniform(arg_keys[3], (TOKENS, TOP), jnp.float32) ** level_of(arg_keys[3], (TOKENS, TOP), ((0, 64),), -0.2, 0.2)), 0.049804688, 1.0).astype(jnp.bfloat16)
    w_gate = centred(arg_keys[4], (EXPERTS, D, FF), D ** -0.5, 0.15625, ((0, 64), (2, 4)))
    w_up = centred(arg_keys[5], (EXPERTS, D, FF), D ** -0.5, 0.15625, ((0, 64), (2, 4)))
    w_down = centred(arg_keys[6], (EXPERTS, FF, D), FF ** -0.5, 0.15625, ((0, 64), (1, 4)))
    return {"tokens": tokens, "out_grad": out_grad, "expert_ids": expert_ids, "combine": combine, "w_gate": w_gate, "w_up": w_up, "w_down": w_down}


ALPHA = 1.702


def expert_rows(rows_x, rows_dy, weight_c, gate_w, up_w, down_w):
    gate_pre = jnp.dot(rows_x, gate_w, preferred_element_type=jnp.float32)
    up_pre = jnp.dot(rows_x, up_w, preferred_element_type=jnp.float32)
    squash = jax.nn.sigmoid(ALPHA * gate_pre)
    glu_out = gate_pre * squash
    activation = (glu_out * (up_pre + 1.0)).astype(jnp.bfloat16)
    back_proj = lax.dot_general(rows_dy, down_w, (((1,), (1,)), ((), ())), preferred_element_type=jnp.float32)
    score_part = jnp.sum(activation.astype(jnp.float32) * back_proj, axis=1)
    weight_col = weight_c.astype(jnp.float32)[:, None]
    scaled_grad = (weight_col * rows_dy.astype(jnp.float32)).astype(jnp.bfloat16)
    act_grad = weight_col * back_proj
    slope = squash + ALPHA * gate_pre * squash * (1.0 - squash)
    gate_grad = (act_grad * (up_pre + 1.0) * slope).astype(jnp.bfloat16)
    up_grad = (act_grad * glu_out).astype(jnp.bfloat16)
    first_dims = (((0,), (0,)), ((), ()))
    down_total = lax.dot_general(activation, scaled_grad, first_dims, preferred_element_type=jnp.float32)
    gate_total = lax.dot_general(rows_x, gate_grad, first_dims, preferred_element_type=jnp.float32)
    up_total = lax.dot_general(rows_x, up_grad, first_dims, preferred_element_type=jnp.float32)
    last_dims = (((1,), (1,)), ((), ()))
    input_grad = lax.dot_general(gate_grad, gate_w, last_dims, preferred_element_type=jnp.float32)
    input_grad = input_grad + lax.dot_general(up_grad, up_w, last_dims, preferred_element_type=jnp.float32)
    return input_grad, score_part, gate_total, up_total, down_total


def reference(tokens, out_grad, expert_ids, combine, w_gate, w_up, w_down):
    assigned = TOKENS * TOP
    flat_ids = expert_ids.reshape(-1).astype(jnp.int32)
    flat_weight = combine.reshape(-1)
    sorted_pairs = jnp.argsort(flat_ids, stable=True).astype(jnp.int32)
    expert_hits = jnp.sum((flat_ids[:, None] == jnp.arange(EXPERTS, dtype=jnp.int32)[None, :]).astype(jnp.int32), axis=0)
    padded_hits = (expert_hits + 127) // 128 * 128
    pad_start = jnp.cumsum(padded_hits).astype(jnp.int32) - padded_hits
    sort_start = jnp.cumsum(expert_hits).astype(jnp.int32) - expert_hits
    block_total = assigned // 128 + EXPERTS

    def scan_step(accumulators, block_index):
        gate_acc, up_acc, down_acc = accumulators
        first_row = block_index * 128
        owner_expert = jnp.sum((pad_start <= first_row).astype(jnp.int32)) - 1
        within = first_row + jnp.arange(128, dtype=jnp.int32) - pad_start[owner_expert]
        valid_rows = within < expert_hits[owner_expert]
        pair_index = sorted_pairs[jnp.clip(sort_start[owner_expert] + within, 0, assigned - 1)]
        token_row = pair_index // TOP
        rows_x = jnp.where(valid_rows[:, None], tokens[token_row], 0.0).astype(tokens.dtype)
        rows_dy = jnp.where(valid_rows[:, None], out_grad[token_row], 0.0).astype(out_grad.dtype)
        weight_c = jnp.where(valid_rows, flat_weight[pair_index], 0.0).astype(combine.dtype)
        input_grad, score_part, gate_total, up_total, down_total = expert_rows(
            rows_x, rows_dy, weight_c, w_gate[owner_expert], w_up[owner_expert], w_down[owner_expert])
        gate_acc = gate_acc.at[owner_expert].add(gate_total)
        up_acc = up_acc.at[owner_expert].add(up_total)
        down_acc = down_acc.at[owner_expert].add(down_total)
        target = jnp.where(valid_rows, pair_index, assigned).astype(jnp.int32)
        return (gate_acc, up_acc, down_acc), (input_grad, score_part, target)

    initial = (jnp.zeros((EXPERTS, D, FF), jnp.float32), jnp.zeros((EXPERTS, D, FF), jnp.float32),
               jnp.zeros((EXPERTS, FF, D), jnp.float32))
    totals, outputs = lax.scan(scan_step, initial, jnp.arange(block_total, dtype=jnp.int32))
    input_grads, score_parts, targets = outputs
    targets = targets.reshape(-1)
    token_targets = jnp.where(targets < assigned, targets // TOP, TOKENS).astype(jnp.int32)
    grad_tokens = jnp.zeros((TOKENS, D), jnp.float32).at[token_targets].add(input_grads.reshape(-1, D), mode="drop")
    grad_combine = jnp.zeros((assigned,), jnp.float32).at[targets].set(score_parts.reshape(-1), mode="drop")
    return (grad_tokens.astype(jnp.bfloat16), grad_combine.reshape(TOKENS, TOP), totals[0], totals[1], totals[2])
```

```python
import functools

import jax
import jax.numpy as jnp
from jax import lax
from jax.experimental import pallas as pl
from jax.experimental.pallas import tpu as pltpu
from jax.sharding import PartitionSpec as P

ALPHA = 1.702
MESH = pl.DeviceIdType.MESH
NX, NY, NZ, NC = 4, 4, 8, 2
CAP = 16
TOP = 4
EARLY = 0
BF16, F32 = jnp.bfloat16, jnp.float32
NT = (((1,), (1,)), ((), ()))
TN = (((0,), (0,)), ((), ()))


def dot(a, b, dims=(((1,), (0,)), ((), ()))):
    return lax.dot_general(a, b, dims, preferred_element_type=F32)


def route_kernel(
    dims, tok_hbm, dy_hbm, meta_ref, wg_hbm, wu_hbm, wd_hbm,
    out_tok, out_score, out_x, out_sg, out_agu,
    zbuf, zmeta, ysend, yrecv, rows_x, rows_dy, wg, wu, wd, sg, agu,
    igb, rs1, rs2s, rs2, yrs, yrr, zrs, zrr, zss, zsr, xss, xsr, pmat,
    in_sem, w_sem, o_sem, e_send, e_recv, z_send, z_recv, zm_send, zm_recv, y_send, y_recv,
    x_send, x_recv, xf_send, xf_recv, r1_send, r1_recv, r2_send, r2_recv,
    yr_send, yr_recv, zr_send, zr_recv, zs_send, zs_recv, xs_send, xs_recv,
):
    tok, dl, ff, early = dims
    late = dl - early
    width = 2 * dl + 2 * (NX - 1) * early
    groups = NY * NC
    rows = groups * CAP
    e = lax.axis_index("expert")
    x = lax.axis_index("etp")
    y = e // (NZ * NC)
    z = lax.rem(e // NC, NZ)
    c = lax.rem(e, NC)
    q = y * NC + c
    xr = lax.rem(x + 1, NX)
    xl = lax.rem(x + NX - 1, NX)
    xo = lax.rem(x + 2, NX)

    def at(y_, z_, c_, x_):
        return ((y_ * NZ + z_) * NC + c_, x_)

    right, left = (e, xr), (e, xl)

    def remote(src, dst, send, recv, dev):
        return pltpu.make_async_remote_copy(
            src_ref=src, dst_ref=dst, send_sem=send, recv_sem=recv, device_id=dev, device_id_type=MESH
        )

    def lanes(start, size):
        return pl.ds(pl.multiple_of(start, 128), size)

    def group_rows(index):
        return pl.ds(pl.multiple_of(index * CAP, CAP), CAP)

    loads = [
        pltpu.make_async_copy(tok_hbm, zbuf.at[0, :, pl.ds(0, dl)], in_sem.at[0]),
        pltpu.make_async_copy(dy_hbm, zbuf.at[0, :, pl.ds(dl, dl)], in_sem.at[1]),
    ]
    weights = [
        pltpu.make_async_copy(wg_hbm, wg, w_sem.at[0]),
        pltpu.make_async_copy(wu_hbm, wu, w_sem.at[1]),
        pltpu.make_async_copy(wd_hbm, wd, w_sem.at[2]),
    ]
    for cp in loads + weights:
        cp.start()

    group_peers = [(dy, dc) for dy in range(NY) for dc in range(NC) if dy or dc]

    def group_peer(dy, dc):
        return lax.rem(y + dy, NY), lax.rem(c + dc, NC)

    barrier = pltpu.get_barrier_semaphore()
    peers = [at(group_peer(dy, dc)[0], z, group_peer(dy, dc)[1], x) for dy, dc in group_peers]
    peers += [(e, lax.rem(x + d, NX)) for d in range(1, NX)]
    peers += [at(y, lax.rem(z + d, NZ), c, x) for d in range(1, NZ)]
    for dev in peers:
        pl.semaphore_signal(barrier, inc=1, device_id=dev, device_id_type=MESH)

    experts = NY * NZ * NC
    ids = meta_ref[0:TOP, :]
    e_iota = lax.broadcasted_iota(jnp.int32, (experts, tok), 0).astype(F32)
    hits = [e_iota == ids[k : k + 1, :] for k in range(TOP)]
    named = functools.reduce(jnp.logical_or, hits)
    named = jnp.where(named, 1.0, 0.0).astype(BF16)
    before = lax.broadcasted_iota(jnp.int32, (tok, tok), 0) < lax.broadcasted_iota(jnp.int32, (tok, tok), 1)
    ranks = dot(named, jnp.where(before, 1.0, 0.0).astype(BF16))
    for k in range(TOP):
        rank = jnp.sum(jnp.where(hits[k], ranks, 0.0), axis=0, keepdims=True)
        zmeta[0, k : k + 1, :] = ids[k : k + 1, :] * CAP + rank
        zmeta[0, TOP + k : TOP + k + 1, :] = meta_ref[TOP + k : TOP + k + 1, :]

    for cp in loads:
        cp.wait()
    pl.semaphore_wait(barrier, len(peers))

    if early:
        copies = []
        for d in range(1, NX):
            base = 2 * dl + (NX - d - 1) * 2 * early
            for part in range(2):
                copies.append(remote(
                    zbuf.at[0, :, pl.ds(part * dl + late, early)],
                    zbuf.at[0, :, pl.ds(base + part * early, early)],
                    e_send.at[d - 1, part], e_recv.at[NX - d - 1, part], (e, lax.rem(x + d, NX)),
                ))
        for cp in copies:
            cp.start()
        for cp in copies:
            cp.wait()

    def z_copies(src, dst, dev):
        return (
            remote(zbuf.at[src], zbuf.at[dst], z_send.at[dst], z_recv.at[dst], dev),
            remote(zmeta.at[src], zmeta.at[dst], zm_send.at[dst], zm_recv.at[dst], dev),
        )

    z_up = at(y, lax.rem(z + 1, NZ), c, x)
    z_down = at(y, lax.rem(z + NZ - 1, NZ), c, x)
    for cp in z_copies(0, 1, z_up):
        cp.start()
    if NZ > 2:
        for cp in z_copies(0, 2, z_down):
            cp.start()

    def hit_masks(i):
        j = lax.broadcasted_iota(jnp.int32, (rows, tok), 0)
        expert = ((j // (CAP * NC)) * NZ + z) * NC + lax.rem(j // CAP, NC)
        code = (expert * CAP + lax.rem(j, CAP)).astype(F32)
        return [code == zmeta[i, k : k + 1, :] for k in range(TOP)]

    def stage_a(i):
        @pl.when(i > 0)
        def _():
            for cp in z_copies(0, i, z_up):
                cp.wait_recv()

        @pl.when((i > 0) & (i + 2 < NZ))
        def _():
            step = 2 * lax.rem(i, 2) - 1
            for cp in z_copies(i, i + 2, at(y, lax.rem(z + step + NZ, NZ), c, x)):
                cp.start()

        masks = hit_masks(i)
        pick = jnp.where(functools.reduce(jnp.logical_or, masks), 1.0, 0.0).astype(BF16)
        pmat[i] = pick
        scale = functools.reduce(
            jnp.add, [jnp.where(masks[k], zmeta[i, TOP + k : TOP + k + 1, :], 0.0) for k in range(TOP)]
        )
        scale = jnp.sum(scale, axis=1, keepdims=True)
        ysend[i, :, 0:width] = dot(pick, zbuf[i]).astype(BF16)
        ysend[i, :, width : width + 128] = jnp.broadcast_to(scale, (rows, 128)).astype(BF16)
        for dy, dc in group_peers:
            yp, cp_ = group_peer(dy, dc)
            remote(
                ysend.at[i, group_rows(yp * NC + cp_)], yrecv.at[i, group_rows(q)],
                y_send.at[i], y_recv.at[i], at(yp, z, cp_, x),
            ).start()
        yrecv[i, group_rows(q), :] = ysend[i, group_rows(q), :]

    others = pl.ds(0, rows - CAP)

    def chunk(i):
        return pl.ds(pl.multiple_of(i * rows, rows), rows)

    def x_copies(i):
        out = []
        for part, buf in enumerate((rows_x, rows_dy)):
            src = yrecv.at[i, :, pl.ds(part * dl, late)]
            dst = buf.at[chunk(i), lanes(x * dl, late)]
            out.append(remote(src, dst, x_send.at[i, part], x_recv.at[i, part], right))
            out.append(remote(src, dst, x_send.at[i, 2 + part], x_recv.at[i, 2 + part], left))
        return out

    def stage_b(i):
        remote(ysend.at[i, others], yrecv.at[i, others], y_send.at[i], y_recv.at[i], right).wait_recv()
        for cp in x_copies(i):
            cp.start()
        for part, buf in enumerate((rows_x, rows_dy)):
            buf[chunk(i), lanes(x * dl, dl)] = yrecv[i, :, part * dl : (part + 1) * dl]
            if early:
                for d in range(1, NX):
                    base = 2 * dl + (d - 1) * 2 * early + part * early
                    buf[chunk(i), lanes(lax.rem(x + d, NX) * dl + late, early)] = yrecv[i, :, base : base + early]

    def forward_copies(i):
        tok_ref = rows_x.at[chunk(i), lanes(xl * dl, late)]
        dy_ref = rows_dy.at[chunk(i), lanes(xr * dl, late)]
        return (
            remote(tok_ref, tok_ref, xf_send.at[i, 0], xf_recv.at[i, 0], right),
            remote(dy_ref, dy_ref, xf_send.at[i, 1], xf_recv.at[i, 1], left),
        )

    def stage_c(i):
        tr, tl, dr, dl_ = x_copies(i)
        fr, fl = forward_copies(i)
        tr.wait_recv()
        fr.start()
        dl_.wait_recv()
        fl.start()

    half = rows // 2
    halves = (pl.ds(0, half), pl.ds(half, half))

    def rs1_copies(i):
        return (
            remote(igb.at[i, halves[0], lanes(xo * dl, dl)], rs1.at[i, 0], r1_send.at[i, 0], r1_recv.at[i, 0], right),
            remote(igb.at[i, halves[1], lanes(xo * dl, dl)], rs1.at[i, 1], r1_send.at[i, 1], r1_recv.at[i, 1], left),
        )

    def stage_d(i):
        tr, tl, dr, dl_ = x_copies(i)
        tl.wait_recv()
        dr.wait_recv()
        for cp in forward_copies(i):
            cp.wait_recv()
        rx = rows_x[chunk(i), :]
        rdy = rows_dy[chunk(i), :]
        gate_pre = dot(rx, wg[...])
        up_one = dot(rx, wu[...]) + 1.0
        back = dot(rdy, wd[...], NT)
        scale = yrecv[i, :, width : width + 128].astype(F32)
        squash = jax.nn.sigmoid(ALPHA * gate_pre)
        glu = gate_pre * squash
        act = (glu * up_one).astype(BF16)
        score = jnp.sum(act.astype(F32) * back, axis=1, keepdims=True)
        score = jnp.broadcast_to(score, (rows, 128))
        top = score.astype(BF16)
        rest = (score - top.astype(F32)).astype(BF16)
        lane = lax.broadcasted_iota(jnp.int32, (rows, 128), 1)
        yrs[i, :, dl : dl + 128] = jnp.where(lane < 64, top.astype(F32), rest.astype(F32)).astype(BF16)
        act_grad = jnp.concatenate([scale] * (ff // 128), axis=1) * back
        slope = squash + ALPHA * gate_pre * squash * (1.0 - squash)
        gate_grad = (act_grad * up_one * slope).astype(BF16)
        up_grad = (act_grad * glu).astype(BF16)
        agu[chunk(i), 0:ff] = act
        agu[chunk(i), ff : 2 * ff] = gate_grad
        agu[chunk(i), 2 * ff : 3 * ff] = up_grad
        sg[chunk(i), :] = (
            jnp.concatenate([scale] * (NX * dl // 128), axis=1) * rdy.astype(F32)
        ).astype(BF16)
        igb[i] = (dot(gate_grad, wg[...], NT) + dot(up_grad, wu[...], NT)).astype(BF16)
        for cp in rs1_copies(i):
            cp.start()

    def rs2_copies(i):
        return (
            remote(rs2s.at[i, 0], rs2.at[i, 0], r2_send.at[i, 0], r2_recv.at[i, 0], right),
            remote(rs2s.at[i, 1], rs2.at[i, 1], r2_send.at[i, 1], r2_recv.at[i, 1], left),
        )

    def stage_e(i):
        first, second = rs1_copies(i)
        to_right, to_left = rs2_copies(i)
        first.wait_recv()
        rs2s[i, 0, halves[0], :] = (
            igb[i, halves[0], lanes(xr * dl, dl)].astype(F32) + rs1[i, 0].astype(F32)
        ).astype(BF16)
        rs2s[i, 0, halves[1], :] = igb[i, halves[1], lanes(xr * dl, dl)]
        to_right.start()
        second.wait_recv()
        rs2s[i, 1, halves[0], :] = igb[i, halves[0], lanes(xl * dl, dl)]
        rs2s[i, 1, halves[1], :] = (
            igb[i, halves[1], lanes(xl * dl, dl)].astype(F32) + rs1[i, 1].astype(F32)
        ).astype(BF16)
        to_left.start()

    def stage_f(i):
        for cp in rs2_copies(i):
            cp.wait_recv()
        total = igb[i, :, lanes(x * dl, dl)].astype(F32) + rs2[i, 0].astype(F32) + rs2[i, 1].astype(F32)
        yrs[i, :, 0:dl] = total.astype(BF16)
        for dy, dc in group_peers:
            yp, cp_ = group_peer(dy, dc)
            remote(
                yrs.at[i, group_rows(yp * NC + cp_)], yrr.at[i, group_rows(q)],
                yr_send.at[i], yr_recv.at[i], at(yp, z, cp_, x),
            ).start()
        yrr[i, group_rows(q), :] = yrs[i, group_rows(q), :]

    def z_back(i):
        step = (lax.rem(i, 2) * -2 + 1) * ((i + 1) // 2)
        dev = at(y, lax.rem(z + step + NZ, NZ), c, x)
        return (
            remote(zrs.at[i], zrr.at[i], zr_send.at[i], zr_recv.at[i], dev),
            remote(zss.at[i], zsr.at[i], zs_send.at[i], zs_recv.at[i], dev),
        )

    def stage_g(i):
        remote(yrs.at[i, others], yrr.at[i, others], yr_send.at[i], yr_recv.at[i], right).wait_recv()
        back = dot(pmat[i], yrr[i, :, 0:dl], TN)
        pair = yrr[i, :, dl : dl + 128].astype(F32)
        score = pair[:, 0:1] + pair[:, 64:65]
        masks = hit_masks(i)
        by_token = [jnp.sum(jnp.where(m, score, 0.0), axis=0, keepdims=True) for m in masks]
        by_token = jnp.concatenate(by_token + [jnp.zeros((8 - TOP, tok), F32)], axis=0)

        @pl.when(i == 0)
        def _():
            zrr[0] = back.astype(BF16)
            zsr[0] = by_token

        @pl.when(i > 0)
        def _():
            zrs[i] = back.astype(BF16)
            zss[i] = by_token
            for cp in z_back(i):
                cp.start()

    outs = [
        pltpu.make_async_copy(rows_x, out_x, o_sem.at[0]),
        pltpu.make_async_copy(sg, out_sg, o_sem.at[1]),
        pltpu.make_async_copy(agu, out_agu, o_sem.at[2]),
    ]

    stages = (stage_a, stage_b, stage_c, stage_d, stage_e, stage_f, stage_g)

    def step(t, carry):
        @pl.when(t == 3)
        def _():
            for cp in weights:
                cp.wait()

        for lag, stage in enumerate(stages):
            @pl.when((t >= lag) & (t < NZ + lag))
            def _():
                stage(t - lag)

            if lag == 3:
                @pl.when(t == NZ + 2)
                def _():
                    for cp in outs:
                        cp.start()
        return carry

    lax.fori_loop(0, NZ + len(stages) - 1, step, 0)

    def finish(i, carry):
        total, score = carry
        for cp in z_back(i):
            cp.wait_recv()
        return total + zrr[i].astype(F32), score + zsr[i]

    total, score = lax.fori_loop(1, NZ, finish, (zrr[0].astype(F32), zsr[0]))
    xss[...] = score
    shares = [
        remote(xss, xsr.at[NX - d - 1], xs_send.at[d - 1], xs_recv.at[NX - d - 1], (e, lax.rem(x + d, NX)))
        for d in range(1, NX)
    ]
    for cp in shares:
        cp.start()
    out_tok[...] = total.astype(BF16)

    def drain(i, carry):
        @pl.when(i > 0)
        def _():
            for cp in z_copies(0, i, z_up) + z_back(i):
                cp.wait_send()

        remote(ysend.at[i, others], yrecv.at[i, others], y_send.at[i], y_recv.at[i], right).wait_send()
        remote(yrs.at[i, others], yrr.at[i, others], yr_send.at[i], yr_recv.at[i], right).wait_send()
        for cp in tuple(x_copies(i)) + forward_copies(i) + rs1_copies(i) + rs2_copies(i):
            cp.wait_send()
        return carry

    lax.fori_loop(0, NZ, drain, 0)
    for cp in outs:
        cp.wait()
    for cp in shares:
        cp.wait()
    for d in range(1, NX):
        score = score + xsr[d - 1]
    out_score[...] = score


def route(tokens, out_grad, meta, w_gate, w_up, w_down):
    tok, dl = tokens.shape
    d, ff = w_gate.shape
    early = EARLY
    width = 2 * dl + 2 * (NX - 1) * early
    rows = NY * NC * CAP
    slots = NZ * rows
    any_spec = pl.BlockSpec(memory_space=pl.ANY)
    vmem = pl.BlockSpec(memory_space=pltpu.VMEM)
    sem = pltpu.SemaphoreType.DMA
    macs = 5 * slots * d * ff
    return pl.pallas_call(
        functools.partial(route_kernel, (tok, dl, ff, early)),
        out_shape=(
            jax.ShapeDtypeStruct((tok, dl), BF16),
            jax.ShapeDtypeStruct((8, tok), F32),
            jax.ShapeDtypeStruct((slots, d), BF16),
            jax.ShapeDtypeStruct((slots, d), BF16),
            jax.ShapeDtypeStruct((slots, 3 * ff), BF16),
        ),
        in_specs=[any_spec, any_spec, vmem, any_spec, any_spec, any_spec],
        out_specs=(vmem, vmem, any_spec, any_spec, any_spec),
        scratch_shapes=[
            pltpu.VMEM((NZ, tok, width), BF16),
            pltpu.VMEM((NZ, 8, tok), F32),
            pltpu.VMEM((NZ, rows, width + 128), BF16),
            pltpu.VMEM((NZ, rows, width + 128), BF16),
            pltpu.VMEM((slots, d), BF16),
            pltpu.VMEM((slots, d), BF16),
            pltpu.VMEM((d, ff), BF16),
            pltpu.VMEM((d, ff), BF16),
            pltpu.VMEM((ff, d), BF16),
            pltpu.VMEM((slots, d), BF16),
            pltpu.VMEM((slots, 3 * ff), BF16),
            pltpu.VMEM((NZ, rows, d), BF16),
            pltpu.VMEM((NZ, 2, rows // 2, dl), BF16),
            pltpu.VMEM((NZ, 2, rows, dl), BF16),
            pltpu.VMEM((NZ, 2, rows, dl), BF16),
            pltpu.VMEM((NZ, rows, dl + 128), BF16),
            pltpu.VMEM((NZ, rows, dl + 128), BF16),
            pltpu.VMEM((NZ, tok, dl), BF16),
            pltpu.VMEM((NZ, tok, dl), BF16),
            pltpu.VMEM((NZ, 8, tok), F32),
            pltpu.VMEM((NZ, 8, tok), F32),
            pltpu.VMEM((8, tok), F32),
            pltpu.VMEM((NX - 1, 8, tok), F32),
            pltpu.VMEM((NZ, rows, tok), BF16),
            sem((2,)), sem((3,)), sem((3,)),
            sem((NX - 1, 2)), sem((NX - 1, 2)),
            sem((NZ,)), sem((NZ,)), sem((NZ,)), sem((NZ,)),
            sem((NZ,)), sem((NZ,)),
            sem((NZ, 4)), sem((NZ, 4)), sem((NZ, 2)), sem((NZ, 2)),
            sem((NZ, 2)), sem((NZ, 2)), sem((NZ, 2)), sem((NZ, 2)),
            sem((NZ,)), sem((NZ,)), sem((NZ,)), sem((NZ,)), sem((NZ,)), sem((NZ,)),
            sem((NX - 1,)), sem((NX - 1,)),
        ],
        compiler_params=pltpu.CompilerParams(
            collective_id=0, has_side_effects=True, vmem_limit_bytes=56 * 2**20
        ),
        cost_estimate=pl.CostEstimate(flops=2 * macs, bytes_accessed=20 * 2**20, transcendentals=0),
        name="route",
    )(tokens, out_grad, meta, w_gate, w_up, w_down)


def weight_kernel(ff, x_ref, sg_ref, agu_ref, gate_ref, up_ref, down_ref):
    both = dot(x_ref[...], agu_ref[:, ff:], TN)
    gate_ref[0] = both[:, :ff]
    up_ref[0] = both[:, ff:]
    down_ref[0] = dot(agu_ref[:, :ff], sg_ref[...], TN)


def weight_grads(rows_x, sg, agu):
    slots, d = rows_x.shape
    ff = agu.shape[1] // 3
    tile = 256
    return pl.pallas_call(
        functools.partial(weight_kernel, ff),
        grid=(d // tile,),
        out_shape=(
            jax.ShapeDtypeStruct((1, d, ff), F32),
            jax.ShapeDtypeStruct((1, d, ff), F32),
            jax.ShapeDtypeStruct((1, ff, d), F32),
        ),
        in_specs=[
            pl.BlockSpec((slots, tile), lambda i: (0, i)),
            pl.BlockSpec((slots, tile), lambda i: (0, i)),
            pl.BlockSpec((slots, 3 * ff), lambda i: (0, 0)),
        ],
        out_specs=(
            pl.BlockSpec((1, tile, ff), lambda i: (0, i, 0)),
            pl.BlockSpec((1, tile, ff), lambda i: (0, i, 0)),
            pl.BlockSpec((1, ff, tile), lambda i: (0, 0, i)),
        ),
        compiler_params=pltpu.CompilerParams(vmem_limit_bytes=48 * 2**20),
        cost_estimate=pl.CostEstimate(
            flops=6 * slots * d * ff, bytes_accessed=16 * 2**20, transcendentals=0
        ),
        name="weight_grads",
    )(rows_x, sg, agu)


def local(tokens, out_grad, expert_ids, combine, w_gate, w_up, w_down):
    meta = jnp.concatenate([expert_ids.astype(F32).T, combine.astype(F32).T], axis=0)
    grad_tokens, score, rows_x, sg, agu = route(tokens, out_grad, meta, w_gate[0], w_up[0], w_down[0])
    gate_total, up_total, down_total = weight_grads(rows_x, sg, agu)
    return grad_tokens, score[:TOP].T, gate_total, up_total, down_total


def solution(mesh):
    return jax.shard_map(
        local,
        mesh=mesh,
        in_specs=(
            P("expert", "etp"),
            P("expert", "etp"),
            P("expert", None),
            P("expert", None),
            P("expert", None, "etp"),
            P("expert", None, "etp"),
            P("expert", "etp", None),
        ),
        out_specs=(
            P("expert", "etp"),
            P("expert", None),
            P("expert", None, "etp"),
            P("expert", None, "etp"),
            P("expert", "etp", None),
        ),
        check_vma=False,
    )
```

```python
import functools

import jax
import jax.numpy as jnp
from jax import lax
from jax.experimental import pallas as pl
from jax.experimental.pallas import tpu as pltpu
from jax.sharding import PartitionSpec as P

ALPHA = 1.702
MESH = pl.DeviceIdType.MESH
NX, NY, NZ, NC = 4, 4, 8, 2
CAP = 16
TOP = 4
EARLY = 128
BF16, F32 = jnp.bfloat16, jnp.float32
ORDER = (
    "A0H0B0A1C0A2B1H1",
    "B2A3C1D0H2B3E0H3",
    "A4C2D1C3A5B4E1A6",
    "H4D3B5A7F1C4D2B6",
    "H5C5F0D4H6B7G0C6",
    "D5E4H7G1C7D6E5F4",
    "E6D7F5E3G4F6E7G5",
    "F3G6E2W0F7G3F2G7",
    "W1W2W3G2W4W5",
)
NT = (((1,), (1,)), ((), ()))
TN = (((0,), (0,)), ((), ()))


def dot(a, b, dims=(((1,), (0,)), ((), ()))):
    return lax.dot_general(a, b, dims, preferred_element_type=F32)


def route_kernel(
    dims, tok_hbm, dy_hbm, ids_ref, combine_ref, wg_hbm, wu_hbm, wd_hbm,
    out_tok, out_score, gate_buf, up_buf, down_buf,
    zbuf, zmeta, ysend, yrecv, hsend, hrecv, rows_x, rows_dy, wgu, wd, sg, gu, x_t, act_t,
    igb, own, rs1, rs2, yrs, yrr, zrs, zrr, zss, zsr, sco, sci, pmat,
    in_sem, w_sem, e_send, e_recv, z_send, z_recv, zm_send, zm_recv, y_send, y_recv, h_send, h_recv,
    x_send, x_recv, xf_send, xf_recv, r1_send, r1_recv, r2_send, r2_recv,
    yr_send, yr_recv, zr_send, zr_recv, zs_send, zs_recv, sc_send, sc_recv,
):
    tok, dl, ff, early = dims
    late = dl - early
    width = 2 * dl + 2 * (NX - 1) * early
    groups = NY * NC
    rows = groups * CAP
    e = lax.axis_index("expert")
    x = lax.axis_index("etp")
    y = e // (NZ * NC)
    z = lax.rem(e // NC, NZ)
    c = lax.rem(e, NC)
    q = y * NC + c
    xr = lax.rem(x + 1, NX)
    xl = lax.rem(x + NX - 1, NX)
    xo = lax.rem(x + 2, NX)

    def at(y_, z_, c_, x_):
        return ((y_ * NZ + z_) * NC + c_, x_)

    right, left = (e, xr), (e, xl)

    def remote(src, dst, send, recv, dev):
        return pltpu.make_async_remote_copy(
            src_ref=src, dst_ref=dst, send_sem=send, recv_sem=recv, device_id=dev, device_id_type=MESH
        )

    def lanes(start, size):
        return pl.ds(pl.multiple_of(start, 128), size)

    def group_rows(index):
        return pl.ds(pl.multiple_of(index * CAP, CAP), CAP)

    loads = [
        pltpu.make_async_copy(tok_hbm, zbuf.at[0, :, pl.ds(0, dl)], in_sem.at[0]),
        pltpu.make_async_copy(dy_hbm, zbuf.at[0, :, pl.ds(dl, dl)], in_sem.at[1]),
    ]
    weights = [
        pltpu.make_async_copy(wg_hbm, wgu.at[:, pl.ds(0, ff)], w_sem.at[0]),
        pltpu.make_async_copy(wu_hbm, wgu.at[:, pl.ds(ff, ff)], w_sem.at[1]),
        pltpu.make_async_copy(wd_hbm, wd, w_sem.at[2]),
    ]
    for cp in loads:
        cp.start()

    group_peers = [(dy, dc) for dy in range(NY) for dc in range(NC) if dy or dc]

    def group_peer(dy, dc):
        return lax.rem(y + dy, NY), lax.rem(c + dc, NC)

    barrier = pltpu.get_barrier_semaphore()
    peers = [(e, lax.rem(x + d, NX)) for d in range(1, NX)]
    peers += [at(y, lax.rem(z + d, NZ), c, x) for d in range(1, NZ)]
    peers += [at(group_peer(dy, dc)[0], z, group_peer(dy, dc)[1], x) for dy, dc in group_peers]
    for dev in peers:
        pl.semaphore_signal(barrier, inc=1, device_id=dev, device_id_type=MESH)
    for cp in weights:
        cp.start()

    experts = NY * NZ * NC
    ids = ids_ref[...].astype(F32)
    e_iota = lax.broadcasted_iota(jnp.int32, (experts, tok), 0).astype(F32)
    hits = [e_iota == ids[k : k + 1, :] for k in range(TOP)]
    named = functools.reduce(jnp.logical_or, hits)
    named = jnp.where(named, 1.0, 0.0).astype(BF16)
    before = lax.broadcasted_iota(jnp.int32, (tok, tok), 0) < lax.broadcasted_iota(jnp.int32, (tok, tok), 1)
    ranks = dot(named, jnp.where(before, 1.0, 0.0).astype(BF16))
    for k in range(TOP):
        rank = jnp.sum(jnp.where(hits[k], ranks, 0.0), axis=0, keepdims=True)
        zmeta[0, k : k + 1, :] = ids[k : k + 1, :] * CAP + rank
    zmeta[0, TOP : 2 * TOP, :] = combine_ref[...].astype(F32)

    for cp in loads:
        cp.wait()
    pl.semaphore_wait(barrier, len(peers))

    early_copies = []
    for d in range(1, NX):
        base = 2 * dl + (NX - d - 1) * 2 * early
        for part in range(2):
            early_copies.append(remote(
                zbuf.at[0, :, pl.ds(part * dl + late, early)],
                zbuf.at[0, :, pl.ds(base + part * early, early)],
                e_send.at[d - 1, part], e_recv.at[NX - d - 1, part], (e, lax.rem(x + d, NX)),
            ))
    for cp in early_copies:
        cp.start()

    z_up = at(y, lax.rem(z + 1, NZ), c, x)
    z_down = at(y, lax.rem(z + NZ - 1, NZ), c, x)

    def z_own(src, dst, dev):
        part = pl.ds(0, 2 * dl)
        return (
            remote(zbuf.at[src, :, part], zbuf.at[dst, :, part], z_send.at[dst, 0], z_recv.at[dst, 0], dev),
            remote(zmeta.at[src], zmeta.at[dst], zm_send.at[dst], zm_recv.at[dst], dev),
        )

    def z_rest(src, dst, dev):
        part = pl.ds(2 * dl, width - 2 * dl)
        return (remote(zbuf.at[src, :, part], zbuf.at[dst, :, part], z_send.at[dst, 1], z_recv.at[dst, 1], dev),)

    for cp in z_own(0, 1, z_up) + z_own(0, 2, z_down):
        cp.start()

    def hit_masks(i):
        j = lax.broadcasted_iota(jnp.int32, (rows, tok), 0)
        expert = ((j // (CAP * NC)) * NZ + z) * NC + lax.rem(j // CAP, NC)
        code = (expert * CAP + lax.rem(j, CAP)).astype(F32)
        return [code == zmeta[i, k : k + 1, :] for k in range(TOP)]

    def to_groups(src, dst, send, recv):
        for dy, dc in group_peers:
            yp, cp_ = group_peer(dy, dc)
            remote(src.at[group_rows(yp * NC + cp_)], dst.at[group_rows(q)], send, recv, at(yp, z, cp_, x)).start()
        dst[group_rows(q), :] = src[group_rows(q), :]

    def from_groups(src, dst, send, recv):
        return remote(src.at[others], dst.at[others], send, recv, right)

    def onward(i):
        return at(y, lax.rem(z + 2 * lax.rem(i, 2) - 1 + NZ, NZ), c, x)

    def stage_a(i):
        @pl.when(i > 0)
        def _():
            for cp in z_own(0, i, z_up):
                cp.wait_recv()

        @pl.when((i > 0) & (i + 2 < NZ - 1))
        def _():
            for cp in z_own(i, i + 2, onward(i)):
                cp.start()

        @pl.when(i == NZ - 3)
        def _():
            for cp in z_own(i, NZ - 1, z_up):
                cp.start()

        masks = hit_masks(i)
        pick = jnp.where(functools.reduce(jnp.logical_or, masks), 1.0, 0.0).astype(BF16)
        pmat[i] = pick
        scale = functools.reduce(
            jnp.add, [jnp.where(masks[k], zmeta[i, TOP + k : TOP + k + 1, :], 0.0) for k in range(TOP)]
        )
        scale = jnp.sum(scale, axis=1, keepdims=True)
        ysend[i, :, 0 : 2 * dl] = dot(pick, zbuf[i, :, 0 : 2 * dl]).astype(BF16)
        ysend[i, :, 2 * dl : 2 * dl + 128] = jnp.broadcast_to(scale, (rows, 128)).astype(BF16)
        to_groups(ysend.at[i], yrecv.at[i], y_send.at[i], y_recv.at[i])

    def stage_h(i):
        @pl.when(i == 0)
        def _():
            for cp in early_copies:
                cp.wait()
            for cp in z_rest(0, 1, z_up) + z_rest(0, 2, z_down):
                cp.start()

        @pl.when(i > 0)
        def _():
            for cp in z_rest(0, i, z_up):
                cp.wait_recv()

        @pl.when((i > 0) & (i + 2 < NZ - 1))
        def _():
            for cp in z_rest(i, i + 2, onward(i)):
                cp.start()

        @pl.when(i == NZ - 2)
        def _():
            for cp in z_rest(i, NZ - 1, z_down):
                cp.start()

        hsend[i] = dot(pmat[i], zbuf[i, :, 2 * dl : width]).astype(BF16)
        to_groups(hsend.at[i], hrecv.at[i], h_send.at[i], h_recv.at[i])

    others = pl.ds(0, rows - CAP)

    def chunk(i):
        return pl.ds(pl.multiple_of(i * rows, rows), rows)

    def x_copies(i):
        out = []
        for part, buf in enumerate((rows_x, rows_dy)):
            src = yrecv.at[i, :, pl.ds(part * dl, late)]
            dst = buf.at[chunk(i), lanes(x * dl, late)]
            out.append(remote(src, dst, x_send.at[i, part], x_recv.at[i, part], right))
            out.append(remote(src, dst, x_send.at[i, 2 + part], x_recv.at[i, 2 + part], left))
        return out

    def stage_b(i):
        from_groups(ysend.at[i], yrecv.at[i], y_send.at[i], y_recv.at[i]).wait_recv()
        for cp in x_copies(i):
            cp.start()
        for part, buf in enumerate((rows_x, rows_dy)):
            buf[chunk(i), lanes(x * dl, dl)] = yrecv[i, :, part * dl : (part + 1) * dl]

    def forward_copies(i):
        tok_ref = rows_x.at[chunk(i), lanes(xl * dl, late)]
        dy_ref = rows_dy.at[chunk(i), lanes(xr * dl, late)]
        return (
            remote(tok_ref, tok_ref, xf_send.at[i, 0], xf_recv.at[i, 0], right),
            remote(dy_ref, dy_ref, xf_send.at[i, 1], xf_recv.at[i, 1], left),
        )

    def stage_c(i):
        tr, tl, dr, dl_ = x_copies(i)
        fr, fl = forward_copies(i)
        tr.wait_recv()
        fr.start()
        dl_.wait_recv()
        fl.start()

    half = rows // 2
    halves = (pl.ds(0, half), pl.ds(half, half))

    def rs1_copies(i):
        return (
            remote(igb.at[i, 2, halves[0]], rs1.at[i, 0], r1_send.at[i, 0], r1_recv.at[i, 0], right),
            remote(igb.at[i, 2, halves[1]], rs1.at[i, 1], r1_send.at[i, 1], r1_recv.at[i, 1], left),
        )

    def diagonal():
        row = lax.broadcasted_iota(jnp.int32, (rows, rows), 0)
        return row == lax.broadcasted_iota(jnp.int32, (rows, rows), 1)

    def score_copies(i):
        return [
            remote(
                sco.at[i], sci.at[i, NX - d - 1], sc_send.at[i, d - 1], sc_recv.at[i, NX - d - 1],
                (e, lax.rem(x + d, NX)),
            )
            for d in range(1, NX)
        ]

    def stage_d(i):
        tr, tl, dr, dl_ = x_copies(i)
        tl.wait_recv()
        dr.wait_recv()
        for cp in forward_copies(i):
            cp.wait_recv()
        from_groups(hsend.at[i], hrecv.at[i], h_send.at[i], h_recv.at[i]).wait_recv()
        for part, buf in enumerate((rows_x, rows_dy)):
            for d in range(1, NX):
                base = (d - 1) * 2 * early + part * early
                buf[chunk(i), lanes(lax.rem(x + d, NX) * dl + late, early)] = hrecv[i, :, base : base + early]
        rx = rows_x[chunk(i), :]
        rdy = rows_dy[chunk(i), :]
        both = dot(rx, wgu[...])
        gate_pre = both[:, 0:ff]
        up_one = both[:, ff:] + 1.0
        back = dot(rdy, wd[...], NT)
        scale = yrecv[i, :, 2 * dl : 2 * dl + 128].astype(F32)
        squash = jax.nn.sigmoid(ALPHA * gate_pre)
        glu = gate_pre * squash
        act = (glu * up_one).astype(BF16)
        act_grad = jnp.concatenate([scale] * (ff // 128), axis=1) * back
        slope = squash + ALPHA * gate_pre * squash * (1.0 - squash)
        gate_grad = (act_grad * up_one * slope).astype(BF16)
        up_grad = (act_grad * glu).astype(BF16)
        grads = jnp.concatenate([gate_grad, up_grad], axis=1)
        gu[chunk(i), :] = grads

        def piece(xd):
            return dot(grads, wgu[pl.ds(pl.multiple_of(xd * dl, 128), dl), :], NT)

        igb[i, 2] = piece(xo).astype(BF16)
        for cp in rs1_copies(i):
            cp.start()
        igb[i, 0] = piece(xr).astype(BF16)
        igb[i, 1] = piece(xl).astype(BF16)
        own[i] = piece(x)
        score = jnp.sum(act.astype(F32) * back, axis=1, keepdims=True)
        score = jnp.sum(jnp.where(diagonal(), score, 0.0), axis=0, keepdims=True)
        sco[i] = jnp.broadcast_to(score, (8, rows))
        for cp in score_copies(i):
            cp.start()
        sg[chunk(i), :] = (
            jnp.concatenate([scale] * (NX * dl // 128), axis=1) * rdy.astype(F32)
        ).astype(BF16)
        x_t[:, chunk(i)] = rx.T
        act_t[:, chunk(i)] = act.T

    def rs2_copies(i):
        return (
            remote(igb.at[i, 0], rs2.at[i, 0], r2_send.at[i, 0], r2_recv.at[i, 0], right),
            remote(igb.at[i, 1], rs2.at[i, 1], r2_send.at[i, 1], r2_recv.at[i, 1], left),
        )

    def stage_e(i):
        for side in range(2):
            rs1_copies(i)[side].wait_recv()
            igb[i, side, halves[side], :] = (
                igb[i, side, halves[side], :].astype(F32) + rs1[i, side].astype(F32)
            ).astype(BF16)
            rs2_copies(i)[side].start()

    def stage_f(i):
        for cp in rs2_copies(i):
            cp.wait_recv()
        total = own[i] + rs2[i, 0].astype(F32) + rs2[i, 1].astype(F32)
        yrs[i, :, 0:dl] = total.astype(BF16)
        for cp in score_copies(i):
            cp.wait_recv()
        score = (sco[i] + sci[i, 0] + sci[i, 1] + sci[i, 2])[0:1, :]
        score = jnp.sum(jnp.where(diagonal(), score, 0.0), axis=1, keepdims=True)
        score = jnp.broadcast_to(score, (rows, 128))
        top = score.astype(BF16).astype(F32)
        lane = lax.broadcasted_iota(jnp.int32, (rows, 128), 1)
        yrs[i, :, dl : dl + 128] = jnp.where(lane < 64, top, score - top).astype(BF16)
        to_groups(yrs.at[i], yrr.at[i], yr_send.at[i], yr_recv.at[i])

    def z_back(i):
        step = (lax.rem(i, 2) * -2 + 1) * ((i + 1) // 2)
        dev = at(y, lax.rem(z + step + NZ, NZ), c, x)
        return (
            remote(zrs.at[i], zrr.at[i], zr_send.at[i], zr_recv.at[i], dev),
            remote(zss.at[i], zsr.at[i], zs_send.at[i], zs_recv.at[i], dev),
        )

    def stage_g(i):
        from_groups(yrs.at[i], yrr.at[i], yr_send.at[i], yr_recv.at[i]).wait_recv()
        back = dot(pmat[i], yrr[i, :, 0:dl], TN)
        pair = yrr[i, :, dl : dl + 128].astype(F32)
        score = pair[:, 0:1] + pair[:, 64:65]
        masks = hit_masks(i)
        by_token = [jnp.sum(jnp.where(m, score, 0.0), axis=0, keepdims=True) for m in masks]
        by_token = jnp.concatenate(by_token + [jnp.zeros((8 - TOP, tok), F32)], axis=0)

        @pl.when(i == 0)
        def _():
            zrr[0] = back.astype(BF16)
            zsr[0] = by_token

        @pl.when(i > 0)
        def _():
            zrs[i] = back.astype(BF16)
            zss[i] = by_token
            for cp in z_back(i):
                cp.start()

    tile = 256
    def stage_w(n):
        part = pl.ds(pl.multiple_of(n * tile, tile), tile)
        both = dot(x_t[part, :], gu[...])
        gate_buf[part, :] = both[:, 0:ff]
        up_buf[part, :] = both[:, ff:]
        down_buf[:, part] = dot(act_t[...], sg[:, part])

    for cp in weights:
        cp.wait()

    stages = dict(
        A=stage_a, B=stage_b, C=stage_c, D=stage_d, E=stage_e, F=stage_f, G=stage_g, H=stage_h, W=stage_w
    )
    names = list(stages)
    joined = "".join(ORDER)
    steps = [joined[n : n + 2] for n in range(0, len(joined), 2)]
    codes = [names.index(p[0]) * 8 + int(p[1]) for p in steps]
    words = [sum(code << (7 * k) for k, code in enumerate(codes[n : n + 4])) for n in range(0, len(codes), 4)]

    def step(s, carry):
        word = jnp.int32(words[0])
        for n in range(1, len(words)):
            word = jnp.where(s // 4 == n, jnp.int32(words[n]), word)
        code = lax.shift_right_logical(word, 7 * lax.rem(s, 4)) & 127
        for n, name in enumerate(names):
            @pl.when(code // 8 == n)
            def _():
                stages[name](lax.rem(code, 8))
        return carry

    lax.fori_loop(0, len(steps), step, 0)

    def finish(i, carry):
        total, score = carry
        for cp in z_back(i):
            cp.wait_recv()
        return total + zrr[i].astype(F32), score + zsr[i]

    total, score = lax.fori_loop(1, NZ, finish, (zrr[0].astype(F32), zsr[0]))
    out_tok[...] = total.astype(BF16)
    out_score[...] = score[0:TOP, :]

    def drain(i, carry):
        @pl.when(i > 0)
        def _():
            for cp in z_own(0, i, z_up) + z_rest(0, i, z_up) + z_back(i):
                cp.wait_send()

        from_groups(ysend.at[i], yrecv.at[i], y_send.at[i], y_recv.at[i]).wait_send()
        from_groups(hsend.at[i], hrecv.at[i], h_send.at[i], h_recv.at[i]).wait_send()
        from_groups(yrs.at[i], yrr.at[i], yr_send.at[i], yr_recv.at[i]).wait_send()
        for cp in (*x_copies(i), *forward_copies(i), *rs1_copies(i), *rs2_copies(i), *score_copies(i)):
            cp.wait_send()
        return carry

    lax.fori_loop(0, NZ, drain, 0)


def route(tokens, out_grad, ids, combine, w_gate, w_up, w_down):
    tok, dl = tokens.shape
    d, ff = w_gate.shape
    early = EARLY
    width = 2 * dl + 2 * (NX - 1) * early
    rows = NY * NC * CAP
    slots = NZ * rows
    any_spec = pl.BlockSpec(memory_space=pl.ANY)
    vmem = pl.BlockSpec(memory_space=pltpu.VMEM)
    sem = pltpu.SemaphoreType.DMA
    return pl.pallas_call(
        functools.partial(route_kernel, (tok, dl, ff, early)),
        out_shape=(
            pltpu.VMEM((tok, dl), BF16),
            pltpu.VMEM((TOP, tok), F32),
            pltpu.VMEM((d, ff), F32),
            pltpu.VMEM((d, ff), F32),
            pltpu.VMEM((ff, d), F32),
        ),
        in_specs=[any_spec, any_spec, vmem, vmem, any_spec, any_spec, any_spec],
        out_specs=(vmem, vmem, vmem, vmem, vmem),
        scratch_shapes=[
            pltpu.VMEM((NZ, tok, width), BF16),
            pltpu.VMEM((NZ, 8, tok), F32),
            pltpu.VMEM((NZ, rows, 2 * dl + 128), BF16),
            pltpu.VMEM((NZ, rows, 2 * dl + 128), BF16),
            pltpu.VMEM((NZ, rows, width - 2 * dl), BF16),
            pltpu.VMEM((NZ, rows, width - 2 * dl), BF16),
            pltpu.VMEM((slots, d), BF16),
            pltpu.VMEM((slots, d), BF16),
            pltpu.VMEM((d, 2 * ff), BF16),
            pltpu.VMEM((ff, d), BF16),
            pltpu.VMEM((slots, d), BF16),
            pltpu.VMEM((slots, 2 * ff), BF16),
            pltpu.VMEM((d, slots), BF16),
            pltpu.VMEM((ff, slots), BF16),
            pltpu.VMEM((NZ, 3, rows, dl), BF16),
            pltpu.VMEM((NZ, rows, dl), F32),
            pltpu.VMEM((NZ, 2, rows // 2, dl), BF16),
            pltpu.VMEM((NZ, 2, rows, dl), BF16),
            pltpu.VMEM((NZ, rows, dl + 128), BF16),
            pltpu.VMEM((NZ, rows, dl + 128), BF16),
            pltpu.VMEM((NZ, tok, dl), BF16),
            pltpu.VMEM((NZ, tok, dl), BF16),
            pltpu.VMEM((NZ, 8, tok), F32),
            pltpu.VMEM((NZ, 8, tok), F32),
            pltpu.VMEM((NZ, 8, rows), F32),
            pltpu.VMEM((NZ, NX - 1, 8, rows), F32),
            pltpu.VMEM((NZ, rows, tok), BF16),
            sem((2,)), sem((3,)),
            sem((NX - 1, 2)), sem((NX - 1, 2)),
            sem((NZ, 2)), sem((NZ, 2)), sem((NZ,)), sem((NZ,)),
            sem((NZ,)), sem((NZ,)), sem((NZ,)), sem((NZ,)),
            sem((NZ, 4)), sem((NZ, 4)), sem((NZ, 2)), sem((NZ, 2)),
            sem((NZ, 2)), sem((NZ, 2)), sem((NZ, 2)), sem((NZ, 2)),
            sem((NZ,)), sem((NZ,)), sem((NZ,)), sem((NZ,)), sem((NZ,)), sem((NZ,)),
            sem((NZ, NX - 1)), sem((NZ, NX - 1)),
        ],
        compiler_params=pltpu.CompilerParams(
            collective_id=0, has_side_effects=True, vmem_limit_bytes=50 * 2**20
        ),
        cost_estimate=pl.CostEstimate(
            flops=16 * slots * d * ff, bytes_accessed=12 * 2**20, transcendentals=0
        ),
        name="route",
    )(tokens, out_grad, ids, combine, w_gate, w_up, w_down)


def place_kernel(pieces, *refs):
    count = len(pieces)
    srcs, dsts, sems = refs[:count], refs[count : 2 * count], refs[2 * count]
    copies = []
    for src, dst, n in zip(srcs, dsts, pieces):
        size = src.shape[0] // n
        for k in range(n):
            part = pl.ds(k * size, size)
            copies.append(pltpu.make_async_copy(src.at[part], dst.at[part], sems.at[len(copies)]))
    for cp in copies:
        cp.start()
    for cp in copies:
        cp.wait()


def place(*arrays):
    pieces = [2 if a.size > 2**17 else 1 for a in arrays]
    return pl.pallas_call(
        functools.partial(place_kernel, pieces),
        out_shape=[jax.ShapeDtypeStruct(a.shape, a.dtype) for a in arrays],
        in_specs=[pl.BlockSpec(memory_space=pltpu.VMEM)] * len(arrays),
        out_specs=[pl.BlockSpec(memory_space=pl.ANY)] * len(arrays),
        scratch_shapes=[pltpu.SemaphoreType.DMA((sum(pieces),))],
        compiler_params=pltpu.CompilerParams(vmem_limit_bytes=4 * 2**20),
        name="place",
    )(*arrays)


def local(tokens, out_grad, expert_ids, combine, w_gate, w_up, w_down):
    results = route(tokens, out_grad, expert_ids.T, combine.T, w_gate[0], w_up[0], w_down[0])
    grad_tokens, score, gate_total, up_total, down_total = place(*results)
    return grad_tokens, score.T, gate_total[None], up_total[None], down_total[None]


def solution(mesh):
    return jax.shard_map(
        local,
        mesh=mesh,
        in_specs=(
            P("expert", "etp"),
            P("expert", "etp"),
            P("expert", None),
            P("expert", None),
            P("expert", None, "etp"),
            P("expert", None, "etp"),
            P("expert", "etp", None),
        ),
        out_specs=(
            P("expert", "etp"),
            P("expert", None),
            P("expert", None, "etp"),
            P("expert", None, "etp"),
            P("expert", "etp", None),
        ),
        check_vma=False,
    )
```

```python
import functools

import jax
import jax.numpy as jnp
from jax import lax
from jax.experimental import pallas as pl
from jax.experimental.pallas import tpu as pltpu
from jax.sharding import PartitionSpec as P

ALPHA = 1.702
MESH = pl.DeviceIdType.MESH
NX, NY, NZ, NC = 4, 4, 8, 2
CAP = 16
TOP = 4
EARLY = 128
BF16, F32 = jnp.bfloat16, jnp.float32
LAST = 1
ORDER = (
    "A1B0A2C0A3B1A4B2",
    "H0B3A5C1C2B4A6H1",
    "B5D0H2C3B6H3A7D1",
    "H4C5C4H5D3C6B7H6",
    "D2D5E3H7D6C7D4E6",
    "F3D7E5W0F6E7G3F5",
    "E2G6F7E4G5E1F2G7",
    "F4E0F1G2W1G4F0G1",
    "W2W3W4W5G0",
)
NT = (((1,), (1,)), ((), ()))
TN = (((0,), (0,)), ((), ()))


def dot(a, b, dims=(((1,), (0,)), ((), ()))):
    return lax.dot_general(a, b, dims, preferred_element_type=F32)


def route_kernel(
    dims, tok_hbm, dy_hbm, ids_ref, combine_ref, wg_hbm, wu_hbm, wd_hbm,
    out_tok, out_score, gate_buf, up_buf, down_buf,
    zbuf, zmeta, ysend, yrecv, hsend, hrecv, rows_x, rows_dy, wgu, wd, sg, gu, x_t, act_t,
    igb, own, rs1, rs2, yrs, yrr, zrs, zrr, zss, zsr, sco, sci, pmat,
    in_sem, w_sem, e_send, e_recv, z_send, z_recv, zm_send, zm_recv, y_send, y_recv, h_send, h_recv,
    x_send, x_recv, xf_send, xf_recv, r1_send, r1_recv, r2_send, r2_recv,
    yr_send, yr_recv, zr_send, zr_recv, zs_send, zs_recv, sc_send, sc_recv,
):
    tok, dl, ff, early = dims
    late = dl - early
    width = 2 * dl + 2 * (NX - 1) * early
    groups = NY * NC
    rows = groups * CAP
    e = lax.axis_index("expert")
    x = lax.axis_index("etp")
    y = e // (NZ * NC)
    z = lax.rem(e // NC, NZ)
    c = lax.rem(e, NC)
    q = y * NC + c
    xr = lax.rem(x + 1, NX)
    xl = lax.rem(x + NX - 1, NX)
    xo = lax.rem(x + 2, NX)

    def at(y_, z_, c_, x_):
        return ((y_ * NZ + z_) * NC + c_, x_)

    right, left = (e, xr), (e, xl)

    def remote(src, dst, send, recv, dev):
        return pltpu.make_async_remote_copy(
            src_ref=src, dst_ref=dst, send_sem=send, recv_sem=recv, device_id=dev, device_id_type=MESH
        )

    def lanes(start, size):
        return pl.ds(pl.multiple_of(start, 128), size)

    def group_rows(index):
        return pl.ds(pl.multiple_of(index * CAP, CAP), CAP)

    loads = [
        pltpu.make_async_copy(tok_hbm, zbuf.at[0, :, pl.ds(0, dl)], in_sem.at[0]),
        pltpu.make_async_copy(dy_hbm, zbuf.at[0, :, pl.ds(dl, dl)], in_sem.at[1]),
    ]
    weights = [
        pltpu.make_async_copy(wg_hbm, wgu.at[:, pl.ds(0, ff)], w_sem.at[0]),
        pltpu.make_async_copy(wu_hbm, wgu.at[:, pl.ds(ff, ff)], w_sem.at[1]),
        pltpu.make_async_copy(wd_hbm, wd, w_sem.at[2]),
    ]
    for cp in loads:
        cp.start()

    group_peers = [(dy, dc) for dy in range(NY) for dc in range(NC) if dy or dc]

    def group_peer(dy, dc):
        return lax.rem(y + dy, NY), lax.rem(c + dc, NC)

    barrier = pltpu.get_barrier_semaphore()
    peers = [(e, lax.rem(x + d, NX)) for d in range(1, NX)]
    peers += [at(y, lax.rem(z + d, NZ), c, x) for d in range(1, NZ)]
    peers += [at(group_peer(dy, dc)[0], z, group_peer(dy, dc)[1], x) for dy, dc in group_peers]
    for dev in peers:
        pl.semaphore_signal(barrier, inc=1, device_id=dev, device_id_type=MESH)
    for cp in weights:
        cp.start()

    experts = NY * NZ * NC
    ids = ids_ref[...].astype(F32)
    e_iota = lax.broadcasted_iota(jnp.int32, (experts, tok), 0).astype(F32)
    hits = [e_iota == ids[k : k + 1, :] for k in range(TOP)]
    named = functools.reduce(jnp.logical_or, hits)
    named = jnp.where(named, 1.0, 0.0).astype(BF16)
    before = lax.broadcasted_iota(jnp.int32, (tok, tok), 0) < lax.broadcasted_iota(jnp.int32, (tok, tok), 1)
    ranks = dot(named, jnp.where(before, 1.0, 0.0).astype(BF16))
    for k in range(TOP):
        rank = jnp.sum(jnp.where(hits[k], ranks, 0.0), axis=0, keepdims=True)
        zmeta[0, k : k + 1, :] = ids[k : k + 1, :] * CAP + rank
    zmeta[0, TOP : 2 * TOP, :] = combine_ref[...].astype(F32)

    def hit_masks(i):
        j = lax.broadcasted_iota(jnp.int32, (rows, tok), 0)
        expert = ((j // (CAP * NC)) * NZ + z) * NC + lax.rem(j // CAP, NC)
        code = (expert * CAP + lax.rem(j, CAP)).astype(F32)
        return [code == zmeta[i, k : k + 1, :] for k in range(TOP)]

    def own_slots(i):
        masks = hit_masks(i)
        pick = jnp.where(functools.reduce(jnp.logical_or, masks), 1.0, 0.0).astype(BF16)
        pmat[i] = pick
        scale = functools.reduce(
            jnp.add, [jnp.where(masks[k], zmeta[i, TOP + k : TOP + k + 1, :], 0.0) for k in range(TOP)]
        )
        scale = jnp.sum(scale, axis=1, keepdims=True)
        ysend[i, :, 0 : 2 * dl] = dot(pick, zbuf[i, :, 0 : 2 * dl]).astype(BF16)
        ysend[i, :, 2 * dl : 2 * dl + 128] = jnp.broadcast_to(scale, (rows, 128)).astype(BF16)

    for cp in loads:
        cp.wait()
    own_slots(0)
    pl.semaphore_wait(barrier, len(peers))

    early_copies = []
    for d in range(1, NX):
        base = 2 * dl + (NX - d - 1) * 2 * early
        for part in range(2):
            early_copies.append(remote(
                zbuf.at[0, :, pl.ds(part * dl + late, early)],
                zbuf.at[0, :, pl.ds(base + part * early, early)],
                e_send.at[d - 1, part], e_recv.at[NX - d - 1, part], (e, lax.rem(x + d, NX)),
            ))
    z_up = at(y, lax.rem(z + 1, NZ), c, x)
    z_down = at(y, lax.rem(z + NZ - 1, NZ), c, x)

    def z_own(src, dst, dev):
        part = pl.ds(0, 2 * dl)
        return (
            remote(zbuf.at[src, :, part], zbuf.at[dst, :, part], z_send.at[dst, 0], z_recv.at[dst, 0], dev),
            remote(zmeta.at[src], zmeta.at[dst], zm_send.at[dst], zm_recv.at[dst], dev),
        )

    def z_rest(src, dst, dev):
        part = pl.ds(2 * dl, width - 2 * dl)
        return (remote(zbuf.at[src, :, part], zbuf.at[dst, :, part], z_send.at[dst, 1], z_recv.at[dst, 1], dev),)


    def to_groups(src, dst, send, recv):
        for dy, dc in group_peers:
            yp, cp_ = group_peer(dy, dc)
            remote(src.at[group_rows(yp * NC + cp_)], dst.at[group_rows(q)], send, recv, at(yp, z, cp_, x)).start()
        dst[group_rows(q), :] = src[group_rows(q), :]

    def from_groups(src, dst, send, recv):
        return remote(src.at[others], dst.at[others], send, recv, right)

    to_groups(ysend.at[0], yrecv.at[0], y_send.at[0], y_recv.at[0])
    for cp in z_own(0, 1, z_up) + z_own(0, 2, z_down):
        cp.start()
    for cp in early_copies:
        cp.start()

    def onward(i):
        return at(y, lax.rem(z + 2 * lax.rem(i, 2) - 1 + NZ, NZ), c, x)

    def stage_a(i):
        for cp in z_own(0, i, z_up):
            cp.wait_recv()

        @pl.when(i + 2 < NZ - 1)
        def _():
            for cp in z_own(i, i + 2, onward(i)):
                cp.start()

        @pl.when(i == NZ - 3)
        def _():
            for cp in z_own(i, NZ - 1, z_up):
                cp.start()

        own_slots(i)
        to_groups(ysend.at[i], yrecv.at[i], y_send.at[i], y_recv.at[i])

    def stage_h(i):
        @pl.when(i == 0)
        def _():
            for cp in early_copies:
                cp.wait()
            for cp in z_rest(0, 1, z_up) + z_rest(0, 2, z_down):
                cp.start()

        @pl.when(i > 0)
        def _():
            for cp in z_rest(0, i, z_up):
                cp.wait_recv()

        @pl.when((i > 0) & (i + 2 < NZ - 1))
        def _():
            for cp in z_rest(i, i + 2, onward(i)):
                cp.start()

        @pl.when(i == NZ - 2)
        def _():
            for cp in z_rest(i, NZ - 1, z_down):
                cp.start()

        hsend[i] = dot(pmat[i], zbuf[i, :, 2 * dl : width]).astype(BF16)
        to_groups(hsend.at[i], hrecv.at[i], h_send.at[i], h_recv.at[i])

    others = pl.ds(0, rows - CAP)

    def chunk(i):
        return pl.ds(pl.multiple_of(i * rows, rows), rows)

    def x_copies(i):
        out = []
        for part, buf in enumerate((rows_x, rows_dy)):
            src = yrecv.at[i, :, pl.ds(part * dl, late)]
            dst = buf.at[chunk(i), lanes(x * dl, late)]
            out.append(remote(src, dst, x_send.at[i, part], x_recv.at[i, part], right))
            out.append(remote(src, dst, x_send.at[i, 2 + part], x_recv.at[i, 2 + part], left))
        return out

    def stage_b(i):
        from_groups(ysend.at[i], yrecv.at[i], y_send.at[i], y_recv.at[i]).wait_recv()
        for cp in x_copies(i):
            cp.start()
        for part, buf in enumerate((rows_x, rows_dy)):
            buf[chunk(i), lanes(x * dl, dl)] = yrecv[i, :, part * dl : (part + 1) * dl]

    def forward_copies(i):
        tok_ref = rows_x.at[chunk(i), lanes(xl * dl, late)]
        dy_ref = rows_dy.at[chunk(i), lanes(xr * dl, late)]
        return (
            remote(tok_ref, tok_ref, xf_send.at[i, 0], xf_recv.at[i, 0], right),
            remote(dy_ref, dy_ref, xf_send.at[i, 1], xf_recv.at[i, 1], left),
        )

    def stage_c(i):
        tr, tl, dr, dl_ = x_copies(i)
        fr, fl = forward_copies(i)
        tr.wait_recv()
        fr.start()
        dl_.wait_recv()
        fl.start()

    half = rows // 2
    halves = (pl.ds(0, half), pl.ds(half, half))

    def rs1_copies(i):
        return (
            remote(igb.at[i, 2, halves[0]], rs1.at[i, 0], r1_send.at[i, 0], r1_recv.at[i, 0], right),
            remote(igb.at[i, 2, halves[1]], rs1.at[i, 1], r1_send.at[i, 1], r1_recv.at[i, 1], left),
        )

    def diagonal():
        row = lax.broadcasted_iota(jnp.int32, (rows, rows), 0)
        return row == lax.broadcasted_iota(jnp.int32, (rows, rows), 1)

    def score_copies(i):
        return [
            remote(
                sco.at[i], sci.at[i, NX - d - 1], sc_send.at[i, d - 1], sc_recv.at[i, NX - d - 1],
                (e, lax.rem(x + d, NX)),
            )
            for d in range(1, NX)
        ]

    def stage_d(i):
        tr, tl, dr, dl_ = x_copies(i)
        tl.wait_recv()
        dr.wait_recv()
        for cp in forward_copies(i):
            cp.wait_recv()
        from_groups(hsend.at[i], hrecv.at[i], h_send.at[i], h_recv.at[i]).wait_recv()
        for part, buf in enumerate((rows_x, rows_dy)):
            for d in range(1, NX):
                base = (d - 1) * 2 * early + part * early
                buf[chunk(i), lanes(lax.rem(x + d, NX) * dl + late, early)] = hrecv[i, :, base : base + early]
        rx = rows_x[chunk(i), :]
        rdy = rows_dy[chunk(i), :]
        both = dot(rx, wgu[...])
        gate_pre = both[:, 0:ff]
        up_one = both[:, ff:] + 1.0
        back = dot(rdy, wd[...], NT)
        scale = yrecv[i, :, 2 * dl : 2 * dl + 128].astype(F32)
        squash = jax.nn.sigmoid(ALPHA * gate_pre)
        glu = gate_pre * squash
        act = (glu * up_one).astype(BF16)
        act_grad = jnp.concatenate([scale] * (ff // 128), axis=1) * back
        slope = squash + ALPHA * gate_pre * squash * (1.0 - squash)
        gate_grad = (act_grad * up_one * slope).astype(BF16)
        up_grad = (act_grad * glu).astype(BF16)
        grads = jnp.concatenate([gate_grad, up_grad], axis=1)
        gu[chunk(i), :] = grads

        def piece(xd):
            return dot(grads, wgu[pl.ds(pl.multiple_of(xd * dl, 128), dl), :], NT)

        igb[i, 2] = piece(xo).astype(BF16)
        for cp in rs1_copies(i):
            cp.start()
        igb[i, 0] = piece(xr).astype(BF16)
        igb[i, 1] = piece(xl).astype(BF16)
        own[i] = piece(x)
        score = jnp.sum(act.astype(F32) * back, axis=1, keepdims=True)
        score = jnp.sum(jnp.where(diagonal(), score, 0.0), axis=0, keepdims=True)
        sco[i] = jnp.broadcast_to(score, (8, rows))
        for cp in score_copies(i):
            cp.start()
        sg[chunk(i), :] = (
            jnp.concatenate([scale] * (NX * dl // 128), axis=1) * rdy.astype(F32)
        ).astype(BF16)
        x_t[:, chunk(i)] = rx.T
        act_t[:, chunk(i)] = act.T

    def rs2_copies(i):
        return (
            remote(igb.at[i, 0], rs2.at[i, 0], r2_send.at[i, 0], r2_recv.at[i, 0], right),
            remote(igb.at[i, 1], rs2.at[i, 1], r2_send.at[i, 1], r2_recv.at[i, 1], left),
        )

    def stage_e(i):
        for side in range(2):
            rs1_copies(i)[side].wait_recv()
            igb[i, side, halves[side], :] = (
                igb[i, side, halves[side], :].astype(F32) + rs1[i, side].astype(F32)
            ).astype(BF16)
            rs2_copies(i)[side].start()

    def stage_f(i):
        for cp in rs2_copies(i):
            cp.wait_recv()
        total = own[i] + rs2[i, 0].astype(F32) + rs2[i, 1].astype(F32)
        yrs[i, :, 0:dl] = total.astype(BF16)
        for cp in score_copies(i):
            cp.wait_recv()
        score = (sco[i] + sci[i, 0] + sci[i, 1] + sci[i, 2])[0:1, :]
        score = jnp.sum(jnp.where(diagonal(), score, 0.0), axis=1, keepdims=True)
        score = jnp.broadcast_to(score, (rows, 128))
        top = score.astype(BF16).astype(F32)
        lane = lax.broadcasted_iota(jnp.int32, (rows, 128), 1)
        yrs[i, :, dl : dl + 128] = jnp.where(lane < 64, top, score - top).astype(BF16)
        to_groups(yrs.at[i], yrr.at[i], yr_send.at[i], yr_recv.at[i])

    def z_back(i):
        step = (lax.rem(i, 2) * -2 + 1) * ((i + 1) // 2)
        dev = at(y, lax.rem(z + step + NZ, NZ), c, x)
        return (
            remote(zrs.at[i], zrr.at[i], zr_send.at[i], zr_recv.at[i], dev),
            remote(zss.at[i], zsr.at[i], zs_send.at[i], zs_recv.at[i], dev),
        )

    def stage_g(i):
        from_groups(yrs.at[i], yrr.at[i], yr_send.at[i], yr_recv.at[i]).wait_recv()
        back = dot(pmat[i], yrr[i, :, 0:dl], TN)
        pair = yrr[i, :, dl : dl + 128].astype(F32)
        score = pair[:, 0:1] + pair[:, 64:65]
        masks = hit_masks(i)
        by_token = [jnp.sum(jnp.where(m, score, 0.0), axis=0, keepdims=True) for m in masks]
        by_token = jnp.concatenate(by_token + [jnp.zeros((8 - TOP, tok), F32)], axis=0)

        @pl.when(i == 0)
        def _():
            zrr[0] = back.astype(BF16)
            zsr[0] = by_token

        @pl.when(i > 0)
        def _():
            zrs[i] = back.astype(BF16)
            zss[i] = by_token
            for cp in z_back(i):
                cp.start()

        @pl.when(i > 0)
        def _():
            for cp in z_own(0, i, z_up) + z_rest(0, i, z_up):
                cp.wait_send()

        from_groups(ysend.at[i], yrecv.at[i], y_send.at[i], y_recv.at[i]).wait_send()
        from_groups(hsend.at[i], hrecv.at[i], h_send.at[i], h_recv.at[i]).wait_send()
        from_groups(yrs.at[i], yrr.at[i], yr_send.at[i], yr_recv.at[i]).wait_send()
        for cp in (*x_copies(i), *forward_copies(i), *rs1_copies(i), *rs2_copies(i), *score_copies(i)):
            cp.wait_send()

    tile = 256
    def stage_w(n):
        part = pl.ds(pl.multiple_of(n * tile, tile), tile)
        both = dot(x_t[part, :], gu[...])
        gate_buf[part, :] = both[:, 0:ff]
        up_buf[part, :] = both[:, ff:]
        down_buf[:, part] = dot(act_t[...], sg[:, part])

    for cp in weights:
        cp.wait()

    stages = dict(
        A=stage_a, B=stage_b, C=stage_c, D=stage_d, E=stage_e, F=stage_f, G=stage_g, H=stage_h, W=stage_w
    )
    names = list(stages)
    joined = "".join(ORDER)
    steps = [joined[n : n + 2] for n in range(0, len(joined), 2)]
    codes = [names.index(p[0]) * 8 + int(p[1]) for p in steps]
    words = [sum(code << (7 * k) for k, code in enumerate(codes[n : n + 4])) for n in range(0, len(codes), 4)]

    def step(s, carry):
        word = jnp.int32(words[0])
        for n in range(1, len(words)):
            word = jnp.where(s // 4 == n, jnp.int32(words[n]), word)
        code = lax.shift_right_logical(word, 7 * lax.rem(s, 4)) & 127
        for n, name in enumerate(names):
            @pl.when(code // 8 == n)
            def _():
                stages[name](lax.rem(code, 8))
        return carry

    lax.fori_loop(0, len(steps), step, 0)

    def finish(p, carry):
        i = jnp.where(p == NZ - 1, LAST, jnp.where(p < LAST, p, p + 1))
        total, score = carry
        for cp in z_back(i):
            cp.wait()
        return total + zrr[i].astype(F32), score + zsr[i]

    total, score = lax.fori_loop(1, NZ, finish, (zrr[0].astype(F32), zsr[0]))
    out_tok[...] = total.astype(BF16)
    out_score[...] = score[0:TOP, :]


def route(tokens, out_grad, ids, combine, w_gate, w_up, w_down):
    tok, dl = tokens.shape
    d, ff = w_gate.shape
    early = EARLY
    width = 2 * dl + 2 * (NX - 1) * early
    rows = NY * NC * CAP
    slots = NZ * rows
    any_spec = pl.BlockSpec(memory_space=pl.ANY)
    vmem = pl.BlockSpec(memory_space=pltpu.VMEM)
    sem = pltpu.SemaphoreType.DMA
    return pl.pallas_call(
        functools.partial(route_kernel, (tok, dl, ff, early)),
        out_shape=(
            pltpu.VMEM((tok, dl), BF16),
            pltpu.VMEM((TOP, tok), F32),
            pltpu.VMEM((d, ff), F32),
            pltpu.VMEM((d, ff), F32),
            pltpu.VMEM((ff, d), F32),
        ),
        in_specs=[any_spec, any_spec, vmem, vmem, any_spec, any_spec, any_spec],
        out_specs=(vmem, vmem, vmem, vmem, vmem),
        scratch_shapes=[
            pltpu.VMEM((NZ, tok, width), BF16),
            pltpu.VMEM((NZ, 8, tok), F32),
            pltpu.VMEM((NZ, rows, 2 * dl + 128), BF16),
            pltpu.VMEM((NZ, rows, 2 * dl + 128), BF16),
            pltpu.VMEM((NZ, rows, width - 2 * dl), BF16),
            pltpu.VMEM((NZ, rows, width - 2 * dl), BF16),
            pltpu.VMEM((slots, d), BF16),
            pltpu.VMEM((slots, d), BF16),
            pltpu.VMEM((d, 2 * ff), BF16),
            pltpu.VMEM((ff, d), BF16),
            pltpu.VMEM((slots, d), BF16),
            pltpu.VMEM((slots, 2 * ff), BF16),
            pltpu.VMEM((d, slots), BF16),
            pltpu.VMEM((ff, slots), BF16),
            pltpu.VMEM((NZ, 3, rows, dl), BF16),
            pltpu.VMEM((NZ, rows, dl), F32),
            pltpu.VMEM((NZ, 2, rows // 2, dl), BF16),
            pltpu.VMEM((NZ, 2, rows, dl), BF16),
            pltpu.VMEM((NZ, rows, dl + 128), BF16),
            pltpu.VMEM((NZ, rows, dl + 128), BF16),
            pltpu.VMEM((NZ, tok, dl), BF16),
            pltpu.VMEM((NZ, tok, dl), BF16),
            pltpu.VMEM((NZ, 8, tok), F32),
            pltpu.VMEM((NZ, 8, tok), F32),
            pltpu.VMEM((NZ, 8, rows), F32),
            pltpu.VMEM((NZ, NX - 1, 8, rows), F32),
            pltpu.VMEM((NZ, rows, tok), BF16),
            sem((2,)), sem((3,)),
            sem((NX - 1, 2)), sem((NX - 1, 2)),
            sem((NZ, 2)), sem((NZ, 2)), sem((NZ,)), sem((NZ,)),
            sem((NZ,)), sem((NZ,)), sem((NZ,)), sem((NZ,)),
            sem((NZ, 4)), sem((NZ, 4)), sem((NZ, 2)), sem((NZ, 2)),
            sem((NZ, 2)), sem((NZ, 2)), sem((NZ, 2)), sem((NZ, 2)),
            sem((NZ,)), sem((NZ,)), sem((NZ,)), sem((NZ,)), sem((NZ,)), sem((NZ,)),
            sem((NZ, NX - 1)), sem((NZ, NX - 1)),
        ],
        compiler_params=pltpu.CompilerParams(
            collective_id=0, has_side_effects=True, vmem_limit_bytes=50 * 2**20
        ),
        cost_estimate=pl.CostEstimate(
            flops=16 * slots * d * ff, bytes_accessed=12 * 2**20, transcendentals=0
        ),
        name="route",
    )(tokens, out_grad, ids, combine, w_gate, w_up, w_down)


def place_kernel(pieces, *refs):
    count = len(pieces)
    srcs, dsts, sems = refs[:count], refs[count : 2 * count], refs[2 * count]
    copies = []
    for src, dst, n in zip(srcs, dsts, pieces):
        size = src.shape[0] // n
        for k in range(n):
            part = pl.ds(k * size, size)
            copies.append(pltpu.make_async_copy(src.at[part], dst.at[part], sems.at[len(copies)]))
    for cp in copies:
        cp.start()
    for cp in copies:
        cp.wait()


def place(*arrays):
    pieces = [2 if a.size > 2**17 else 1 for a in arrays]
    return pl.pallas_call(
        functools.partial(place_kernel, pieces),
        out_shape=[jax.ShapeDtypeStruct(a.shape, a.dtype) for a in arrays],
        in_specs=[pl.BlockSpec(memory_space=pltpu.VMEM)] * len(arrays),
        out_specs=[pl.BlockSpec(memory_space=pl.ANY)] * len(arrays),
        scratch_shapes=[pltpu.SemaphoreType.DMA((sum(pieces),))],
        compiler_params=pltpu.CompilerParams(vmem_limit_bytes=4 * 2**20),
        name="place",
    )(*arrays)


def local(tokens, out_grad, expert_ids, combine, w_gate, w_up, w_down):
    results = route(tokens, out_grad, expert_ids.T, combine.T, w_gate[0], w_up[0], w_down[0])
    grad_tokens, score, gate_total, up_total, down_total = place(*results)
    return grad_tokens, score.T, gate_total[None], up_total[None], down_total[None]


def solution(mesh):
    return jax.shard_map(
        local,
        mesh=mesh,
        in_specs=(
            P("expert", "etp"),
            P("expert", "etp"),
            P("expert", None),
            P("expert", None),
            P("expert", None, "etp"),
            P("expert", None, "etp"),
            P("expert", "etp", None),
        ),
        out_specs=(
            P("expert", "etp"),
            P("expert", None),
            P("expert", None, "etp"),
            P("expert", None, "etp"),
            P("expert", "etp", None),
        ),
        check_vma=False,
    )
```

```python
import functools

import jax
import jax.numpy as jnp
from jax import lax
from jax.experimental import pallas as pl
from jax.experimental.pallas import tpu as pltpu
from jax.sharding import PartitionSpec as P

ALPHA = 1.702
MESH = pl.DeviceIdType.MESH
NX, NY, NZ, NC = 4, 4, 8, 2
CAP = 16
TOP = 4
EARLY = 128
BF16, F32 = jnp.bfloat16, jnp.float32
LAST = 2
ORDER = (
    "B0A1A2C0A3B1B2A4",
    "H0B3A5C1H1B4C2A6",
    "B5H2C3D1C4B6H3H4",
    "E1C5A7H5C6D4B7H6",
    "D5E4D6F1C7H7E5F4",
    "D3E6G1D7G4F5E3D2",
    "F6E7G5D0G6F3E2W0",
    "F7W1E0W2G3F2G7W3",
    "F0W4W5G2G0",
)
NT = (((1,), (1,)), ((), ()))
TN = (((0,), (0,)), ((), ()))


def dot(a, b, dims=(((1,), (0,)), ((), ()))):
    return lax.dot_general(a, b, dims, preferred_element_type=F32)


def route_kernel(
    dims, tok_hbm, dy_hbm, ids_ref, combine_ref, wg_hbm, wu_hbm, wd_hbm,
    out_tok, out_score, gate_buf, up_buf, down_buf,
    zbuf, zmeta, ysend, yrecv, hsend, hrecv, rows_x, rows_dy, wgu, wd, sg, gu, x_t, act_t,
    igb, own, rs1, rs2, yrs, yrr, zrs, zrr, zss, zsr, sco, sci, pmat,
    in_sem, w_sem, e_send, e_recv, z_send, z_recv, zm_send, zm_recv, y_send, y_recv, h_send, h_recv,
    x_send, x_recv, xf_send, xf_recv, r1_send, r1_recv, r2_send, r2_recv,
    yr_send, yr_recv, zr_send, zr_recv, zs_send, zs_recv, sc_send, sc_recv,
):
    tok, dl, ff, early = dims
    late = dl - early
    width = 2 * dl + 2 * (NX - 1) * early
    groups = NY * NC
    rows = groups * CAP
    e = lax.axis_index("expert")
    x = lax.axis_index("etp")
    y = e // (NZ * NC)
    z = lax.rem(e // NC, NZ)
    c = lax.rem(e, NC)
    q = y * NC + c
    xr = lax.rem(x + 1, NX)
    xl = lax.rem(x + NX - 1, NX)
    xo = lax.rem(x + 2, NX)

    def at(y_, z_, c_, x_):
        return ((y_ * NZ + z_) * NC + c_, x_)

    right, left = (e, xr), (e, xl)

    def remote(src, dst, send, recv, dev):
        return pltpu.make_async_remote_copy(
            src_ref=src, dst_ref=dst, send_sem=send, recv_sem=recv, device_id=dev, device_id_type=MESH
        )

    def lanes(start, size):
        return pl.ds(pl.multiple_of(start, 128), size)

    def group_rows(index):
        return pl.ds(pl.multiple_of(index * CAP, CAP), CAP)

    loads = [
        pltpu.make_async_copy(tok_hbm, zbuf.at[0, :, pl.ds(0, dl)], in_sem.at[0]),
        pltpu.make_async_copy(dy_hbm, zbuf.at[0, :, pl.ds(dl, dl)], in_sem.at[1]),
    ]
    weights = [
        pltpu.make_async_copy(wg_hbm, wgu.at[:, pl.ds(0, ff)], w_sem.at[0]),
        pltpu.make_async_copy(wu_hbm, wgu.at[:, pl.ds(ff, ff)], w_sem.at[1]),
        pltpu.make_async_copy(wd_hbm, wd, w_sem.at[2]),
    ]
    for cp in loads:
        cp.start()

    group_peers = [(dy, dc) for dy in range(NY) for dc in range(NC) if dy or dc]

    def group_peer(dy, dc):
        return lax.rem(y + dy, NY), lax.rem(c + dc, NC)

    barrier = pltpu.get_barrier_semaphore()
    peers = [(e, lax.rem(x + d, NX)) for d in range(1, NX)]
    peers += [at(y, lax.rem(z + d, NZ), c, x) for d in (1, NZ - 1)]
    peers += [at(group_peer(dy, dc)[0], z, group_peer(dy, dc)[1], x) for dy, dc in group_peers]
    for dev in peers:
        pl.semaphore_signal(barrier, inc=1, device_id=dev, device_id_type=MESH)
    for cp in weights:
        cp.start()

    experts = NY * NZ * NC
    ids = ids_ref[...].astype(F32)
    e_iota = lax.broadcasted_iota(jnp.int32, (experts, tok), 0).astype(F32)
    hits = [e_iota == ids[k : k + 1, :] for k in range(TOP)]
    named = functools.reduce(jnp.logical_or, hits)
    named = jnp.where(named, 1.0, 0.0).astype(BF16)
    before = lax.broadcasted_iota(jnp.int32, (tok, tok), 0) < lax.broadcasted_iota(jnp.int32, (tok, tok), 1)
    ranks = dot(named, jnp.where(before, 1.0, 0.0).astype(BF16))
    for k in range(TOP):
        rank = jnp.sum(jnp.where(hits[k], ranks, 0.0), axis=0, keepdims=True)
        zmeta[0, k : k + 1, :] = ids[k : k + 1, :] * CAP + rank
    zmeta[0, TOP : 2 * TOP, :] = combine_ref[...].astype(F32)

    def hit_masks(i):
        j = lax.broadcasted_iota(jnp.int32, (rows, tok), 0)
        expert = ((j // (CAP * NC)) * NZ + z) * NC + lax.rem(j // CAP, NC)
        code = (expert * CAP + lax.rem(j, CAP)).astype(F32)
        return [code == zmeta[i, k : k + 1, :] for k in range(TOP)]

    def own_slots(i):
        masks = hit_masks(i)
        pick = jnp.where(functools.reduce(jnp.logical_or, masks), 1.0, 0.0).astype(BF16)
        pmat[i] = pick
        scale = functools.reduce(
            jnp.add, [jnp.where(masks[k], zmeta[i, TOP + k : TOP + k + 1, :], 0.0) for k in range(TOP)]
        )
        scale = jnp.sum(scale, axis=1, keepdims=True)
        ysend[i, :, 0 : 2 * dl] = dot(pick, zbuf[i, :, 0 : 2 * dl]).astype(BF16)
        ysend[i, :, 2 * dl : 2 * dl + 128] = jnp.broadcast_to(scale, (rows, 128)).astype(BF16)

    for cp in loads:
        cp.wait()
    own_slots(0)
    pl.semaphore_wait(barrier, len(peers))

    early_copies = []
    for d in range(1, NX):
        base = 2 * dl + (NX - d - 1) * 2 * early
        for part in range(2):
            early_copies.append(remote(
                zbuf.at[0, :, pl.ds(part * dl + late, early)],
                zbuf.at[0, :, pl.ds(base + part * early, early)],
                e_send.at[d - 1, part], e_recv.at[NX - d - 1, part], (e, lax.rem(x + d, NX)),
            ))
    z_up = at(y, lax.rem(z + 1, NZ), c, x)
    z_down = at(y, lax.rem(z + NZ - 1, NZ), c, x)

    def z_own(src, dst, dev):
        part = pl.ds(0, 2 * dl)
        return (
            remote(zbuf.at[src, :, part], zbuf.at[dst, :, part], z_send.at[dst, 0], z_recv.at[dst, 0], dev),
            remote(zmeta.at[src], zmeta.at[dst], zm_send.at[dst], zm_recv.at[dst], dev),
        )

    def z_rest(src, dst, dev):
        part = pl.ds(2 * dl, width - 2 * dl)
        return (remote(zbuf.at[src, :, part], zbuf.at[dst, :, part], z_send.at[dst, 1], z_recv.at[dst, 1], dev),)


    def to_groups(src, dst, send, recv):
        for dy, dc in group_peers:
            yp, cp_ = group_peer(dy, dc)
            remote(src.at[group_rows(yp * NC + cp_)], dst.at[group_rows(q)], send, recv, at(yp, z, cp_, x)).start()
        dst[group_rows(q), :] = src[group_rows(q), :]

    def from_groups(src, dst, send, recv):
        return remote(src.at[others], dst.at[others], send, recv, right)

    to_groups(ysend.at[0], yrecv.at[0], y_send.at[0], y_recv.at[0])
    for cp in z_own(0, 1, z_up) + z_own(0, 2, z_down):
        cp.start()
    for cp in early_copies:
        cp.start()

    def onward(i):
        return at(y, lax.rem(z + 2 * lax.rem(i, 2) - 1 + NZ, NZ), c, x)

    def stage_a(i):
        for cp in z_own(0, i, z_up):
            cp.wait_recv()

        @pl.when(i + 2 < NZ - 1)
        def _():
            for cp in z_own(i, i + 2, onward(i)):
                cp.start()

        @pl.when(i == NZ - 3)
        def _():
            for cp in z_own(i, NZ - 1, z_up):
                cp.start()

        own_slots(i)
        to_groups(ysend.at[i], yrecv.at[i], y_send.at[i], y_recv.at[i])

    def stage_h(i):
        @pl.when(i == 0)
        def _():
            for cp in early_copies:
                cp.wait()
            for cp in z_rest(0, 1, z_up) + z_rest(0, 2, z_down):
                cp.start()

        @pl.when(i > 0)
        def _():
            for cp in z_rest(0, i, z_up):
                cp.wait_recv()

        @pl.when((i > 0) & (i + 2 < NZ - 1))
        def _():
            for cp in z_rest(i, i + 2, onward(i)):
                cp.start()

        @pl.when(i == NZ - 2)
        def _():
            for cp in z_rest(i, NZ - 1, z_down):
                cp.start()

        hsend[i] = dot(pmat[i], zbuf[i, :, 2 * dl : width]).astype(BF16)
        to_groups(hsend.at[i], hrecv.at[i], h_send.at[i], h_recv.at[i])

    others = pl.ds(0, rows - CAP)

    def chunk(i):
        return pl.ds(pl.multiple_of(i * rows, rows), rows)

    def x_copies(i):
        out = []
        for part, buf in enumerate((rows_x, rows_dy)):
            src = yrecv.at[i, :, pl.ds(part * dl, late)]
            dst = buf.at[chunk(i), lanes(x * dl, late)]
            out.append(remote(src, dst, x_send.at[i, part], x_recv.at[i, part], right))
            out.append(remote(src, dst, x_send.at[i, 2 + part], x_recv.at[i, 2 + part], left))
        return out

    def stage_b(i):
        from_groups(ysend.at[i], yrecv.at[i], y_send.at[i], y_recv.at[i]).wait_recv()
        for cp in x_copies(i):
            cp.start()
        for part, buf in enumerate((rows_x, rows_dy)):
            buf[chunk(i), lanes(x * dl, dl)] = yrecv[i, :, part * dl : (part + 1) * dl]

    def forward_copies(i):
        tok_ref = rows_x.at[chunk(i), lanes(xl * dl, late)]
        dy_ref = rows_dy.at[chunk(i), lanes(xr * dl, late)]
        return (
            remote(tok_ref, tok_ref, xf_send.at[i, 0], xf_recv.at[i, 0], right),
            remote(dy_ref, dy_ref, xf_send.at[i, 1], xf_recv.at[i, 1], left),
        )

    def stage_c(i):
        tr, tl, dr, dl_ = x_copies(i)
        fr, fl = forward_copies(i)
        tr.wait_recv()
        fr.start()
        dl_.wait_recv()
        fl.start()

    half = rows // 2
    halves = (pl.ds(0, half), pl.ds(half, half))

    def rs1_copies(i):
        return (
            remote(igb.at[i, 2, halves[0]], rs1.at[i, 0], r1_send.at[i, 0], r1_recv.at[i, 0], right),
            remote(igb.at[i, 2, halves[1]], rs1.at[i, 1], r1_send.at[i, 1], r1_recv.at[i, 1], left),
        )

    def diagonal():
        row = lax.broadcasted_iota(jnp.int32, (rows, rows), 0)
        return row == lax.broadcasted_iota(jnp.int32, (rows, rows), 1)

    def score_copies(i):
        return [
            remote(
                sco.at[i], sci.at[i, NX - d - 1], sc_send.at[i, d - 1], sc_recv.at[i, NX - d - 1],
                (e, lax.rem(x + d, NX)),
            )
            for d in range(1, NX)
        ]

    def stage_d(i):
        tr, tl, dr, dl_ = x_copies(i)
        tl.wait_recv()
        dr.wait_recv()
        for cp in forward_copies(i):
            cp.wait_recv()
        from_groups(hsend.at[i], hrecv.at[i], h_send.at[i], h_recv.at[i]).wait_recv()
        for part, buf in enumerate((rows_x, rows_dy)):
            for d in range(1, NX):
                base = (d - 1) * 2 * early + part * early
                buf[chunk(i), lanes(lax.rem(x + d, NX) * dl + late, early)] = hrecv[i, :, base : base + early]
        rx = rows_x[chunk(i), :]
        rdy = rows_dy[chunk(i), :]
        both = dot(rx, wgu[...])
        gate_pre = both[:, 0:ff]
        up_one = both[:, ff:] + 1.0
        back = dot(rdy, wd[...], NT)
        scale = yrecv[i, :, 2 * dl : 2 * dl + 128].astype(F32)
        squash = jax.nn.sigmoid(ALPHA * gate_pre)
        glu = gate_pre * squash
        act = (glu * up_one).astype(BF16)
        act_grad = jnp.concatenate([scale] * (ff // 128), axis=1) * back
        slope = squash + ALPHA * gate_pre * squash * (1.0 - squash)
        gate_grad = (act_grad * up_one * slope).astype(BF16)
        up_grad = (act_grad * glu).astype(BF16)
        grads = jnp.concatenate([gate_grad, up_grad], axis=1)
        gu[chunk(i), :] = grads

        def piece(xd):
            return dot(grads, wgu[pl.ds(pl.multiple_of(xd * dl, 128), dl), :], NT)

        igb[i, 2] = piece(xo).astype(BF16)
        for cp in rs1_copies(i):
            cp.start()
        igb[i, 0] = piece(xr).astype(BF16)
        igb[i, 1] = piece(xl).astype(BF16)
        own[i] = piece(x)
        score = jnp.sum(act.astype(F32) * back, axis=1, keepdims=True)
        score = jnp.sum(jnp.where(diagonal(), score, 0.0), axis=0, keepdims=True)
        sco[i] = jnp.broadcast_to(score, (8, rows))
        for cp in score_copies(i):
            cp.start()
        sg[chunk(i), :] = (
            jnp.concatenate([scale] * (NX * dl // 128), axis=1) * rdy.astype(F32)
        ).astype(BF16)
        x_t[:, chunk(i)] = rx.T
        act_t[:, chunk(i)] = act.T

    def rs2_copies(i):
        return (
            remote(igb.at[i, 0], rs2.at[i, 0], r2_send.at[i, 0], r2_recv.at[i, 0], right),
            remote(igb.at[i, 1], rs2.at[i, 1], r2_send.at[i, 1], r2_recv.at[i, 1], left),
        )

    def stage_e(i):
        for side in range(2):
            rs1_copies(i)[side].wait_recv()
            igb[i, side, halves[side], :] = (
                igb[i, side, halves[side], :].astype(F32) + rs1[i, side].astype(F32)
            ).astype(BF16)
            rs2_copies(i)[side].start()

    def stage_f(i):
        for cp in rs2_copies(i):
            cp.wait_recv()
        total = own[i] + rs2[i, 0].astype(F32) + rs2[i, 1].astype(F32)
        yrs[i, :, 0:dl] = total.astype(BF16)
        for cp in score_copies(i):
            cp.wait_recv()
        score = (sco[i] + sci[i, 0] + sci[i, 1] + sci[i, 2])[0:1, :]
        score = jnp.sum(jnp.where(diagonal(), score, 0.0), axis=1, keepdims=True)
        score = jnp.broadcast_to(score, (rows, 128))
        top = score.astype(BF16).astype(F32)
        lane = lax.broadcasted_iota(jnp.int32, (rows, 128), 1)
        yrs[i, :, dl : dl + 128] = jnp.where(lane < 64, top, score - top).astype(BF16)
        to_groups(yrs.at[i], yrr.at[i], yr_send.at[i], yr_recv.at[i])

    def z_back(i):
        step = (lax.rem(i, 2) * -2 + 1) * ((i + 1) // 2)
        dev = at(y, lax.rem(z + step + NZ, NZ), c, x)
        return (
            remote(zrs.at[i], zrr.at[i], zr_send.at[i], zr_recv.at[i], dev),
            remote(zss.at[i], zsr.at[i], zs_send.at[i], zs_recv.at[i], dev),
        )

    def stage_g(i):
        from_groups(yrs.at[i], yrr.at[i], yr_send.at[i], yr_recv.at[i]).wait_recv()
        back = dot(pmat[i], yrr[i, :, 0:dl], TN)
        pair = yrr[i, :, dl : dl + 128].astype(F32)
        score = pair[:, 0:1] + pair[:, 64:65]
        masks = hit_masks(i)
        by_token = [jnp.sum(jnp.where(m, score, 0.0), axis=0, keepdims=True) for m in masks]
        by_token = jnp.concatenate(by_token + [jnp.zeros((8 - TOP, tok), F32)], axis=0)

        @pl.when(i == 0)
        def _():
            zrr[0] = back.astype(BF16)
            zsr[0] = by_token

        @pl.when(i > 0)
        def _():
            zrs[i] = back.astype(BF16)
            zss[i] = by_token
            for cp in z_back(i):
                cp.start()

        @pl.when(i > 0)
        def _():
            for cp in z_own(0, i, z_up) + z_rest(0, i, z_up):
                cp.wait_send()

        from_groups(ysend.at[i], yrecv.at[i], y_send.at[i], y_recv.at[i]).wait_send()
        from_groups(hsend.at[i], hrecv.at[i], h_send.at[i], h_recv.at[i]).wait_send()
        from_groups(yrs.at[i], yrr.at[i], yr_send.at[i], yr_recv.at[i]).wait_send()
        for cp in (*x_copies(i), *forward_copies(i), *rs1_copies(i), *rs2_copies(i), *score_copies(i)):
            cp.wait_send()

    tile = 256
    def stage_w(n):
        part = pl.ds(pl.multiple_of(n * tile, tile), tile)
        both = dot(x_t[part, :], gu[...])
        gate_buf[part, :] = both[:, 0:ff]
        up_buf[part, :] = both[:, ff:]
        down_buf[:, part] = dot(act_t[...], sg[:, part])

    for cp in weights:
        cp.wait()

    stages = dict(
        A=stage_a, B=stage_b, C=stage_c, D=stage_d, E=stage_e, F=stage_f, G=stage_g, H=stage_h, W=stage_w
    )
    names = list(stages)
    joined = "".join(ORDER)
    steps = [joined[n : n + 2] for n in range(0, len(joined), 2)]
    codes = [names.index(p[0]) * 8 + int(p[1]) for p in steps]
    words = [sum(code << (7 * k) for k, code in enumerate(codes[n : n + 4])) for n in range(0, len(codes), 4)]

    def step(s, carry):
        word = jnp.int32(words[0])
        for n in range(1, len(words)):
            word = jnp.where(s // 4 == n, jnp.int32(words[n]), word)
        code = lax.shift_right_logical(word, 7 * lax.rem(s, 4)) & 127
        for n, name in enumerate(names):
            @pl.when(code // 8 == n)
            def _():
                stages[name](lax.rem(code, 8))
        return carry

    lax.fori_loop(0, len(steps), step, 0)

    def finish(p, carry):
        i = jnp.where(p == NZ - 1, LAST, jnp.where(p < LAST, p, p + 1))
        total, score = carry
        for cp in z_back(i):
            cp.wait()
        return total + zrr[i].astype(F32), score + zsr[i]

    total, score = lax.fori_loop(1, NZ, finish, (zrr[0].astype(F32), zsr[0]))
    out_tok[...] = total.astype(BF16)
    out_score[...] = score[0:TOP, :]


def route(tokens, out_grad, ids, combine, w_gate, w_up, w_down):
    tok, dl = tokens.shape
    d, ff = w_gate.shape
    early = EARLY
    width = 2 * dl + 2 * (NX - 1) * early
    rows = NY * NC * CAP
    slots = NZ * rows
    any_spec = pl.BlockSpec(memory_space=pl.ANY)
    vmem = pl.BlockSpec(memory_space=pltpu.VMEM)
    sem = pltpu.SemaphoreType.DMA
    return pl.pallas_call(
        functools.partial(route_kernel, (tok, dl, ff, early)),
        out_shape=(
            pltpu.VMEM((tok, dl), BF16),
            pltpu.VMEM((TOP, tok), F32),
            pltpu.VMEM((d, ff), F32),
            pltpu.VMEM((d, ff), F32),
            pltpu.VMEM((ff, d), F32),
        ),
        in_specs=[any_spec, any_spec, vmem, vmem, any_spec, any_spec, any_spec],
        out_specs=(vmem, vmem, vmem, vmem, vmem),
        scratch_shapes=[
            pltpu.VMEM((NZ, tok, width), BF16),
            pltpu.VMEM((NZ, 8, tok), F32),
            pltpu.VMEM((NZ, rows, 2 * dl + 128), BF16),
            pltpu.VMEM((NZ, rows, 2 * dl + 128), BF16),
            pltpu.VMEM((NZ, rows, width - 2 * dl), BF16),
            pltpu.VMEM((NZ, rows, width - 2 * dl), BF16),
            pltpu.VMEM((slots, d), BF16),
            pltpu.VMEM((slots, d), BF16),
            pltpu.VMEM((d, 2 * ff), BF16),
            pltpu.VMEM((ff, d), BF16),
            pltpu.VMEM((slots, d), BF16),
            pltpu.VMEM((slots, 2 * ff), BF16),
            pltpu.VMEM((d, slots), BF16),
            pltpu.VMEM((ff, slots), BF16),
            pltpu.VMEM((NZ, 3, rows, dl), BF16),
            pltpu.VMEM((NZ, rows, dl), F32),
            pltpu.VMEM((NZ, 2, rows // 2, dl), BF16),
            pltpu.VMEM((NZ, 2, rows, dl), BF16),
            pltpu.VMEM((NZ, rows, dl + 128), BF16),
            pltpu.VMEM((NZ, rows, dl + 128), BF16),
            pltpu.VMEM((NZ, tok, dl), BF16),
            pltpu.VMEM((NZ, tok, dl), BF16),
            pltpu.VMEM((NZ, 8, tok), F32),
            pltpu.VMEM((NZ, 8, tok), F32),
            pltpu.VMEM((NZ, 8, rows), F32),
            pltpu.VMEM((NZ, NX - 1, 8, rows), F32),
            pltpu.VMEM((NZ, rows, tok), BF16),
            sem((2,)), sem((3,)),
            sem((NX - 1, 2)), sem((NX - 1, 2)),
            sem((NZ, 2)), sem((NZ, 2)), sem((NZ,)), sem((NZ,)),
            sem((NZ,)), sem((NZ,)), sem((NZ,)), sem((NZ,)),
            sem((NZ, 4)), sem((NZ, 4)), sem((NZ, 2)), sem((NZ, 2)),
            sem((NZ, 2)), sem((NZ, 2)), sem((NZ, 2)), sem((NZ, 2)),
            sem((NZ,)), sem((NZ,)), sem((NZ,)), sem((NZ,)), sem((NZ,)), sem((NZ,)),
            sem((NZ, NX - 1)), sem((NZ, NX - 1)),
        ],
        compiler_params=pltpu.CompilerParams(
            collective_id=0, has_side_effects=True, vmem_limit_bytes=50 * 2**20
        ),
        cost_estimate=pl.CostEstimate(
            flops=16 * slots * d * ff, bytes_accessed=12 * 2**20, transcendentals=0
        ),
        name="route",
    )(tokens, out_grad, ids, combine, w_gate, w_up, w_down)


def place_kernel(pieces, *refs):
    count = len(pieces)
    srcs, dsts, sems = refs[:count], refs[count : 2 * count], refs[2 * count]
    copies = []
    for src, dst, n in zip(srcs, dsts, pieces):
        size = src.shape[0] // n
        for k in range(n):
            part = pl.ds(k * size, size)
            copies.append(pltpu.make_async_copy(src.at[part], dst.at[part], sems.at[len(copies)]))
    for cp in copies:
        cp.start()
    for cp in copies:
        cp.wait()


def place(*arrays):
    pieces = [2 if a.size > 2**17 else 1 for a in arrays]
    return pl.pallas_call(
        functools.partial(place_kernel, pieces),
        out_shape=[jax.ShapeDtypeStruct(a.shape, a.dtype) for a in arrays],
        in_specs=[pl.BlockSpec(memory_space=pltpu.VMEM)] * len(arrays),
        out_specs=[pl.BlockSpec(memory_space=pl.ANY)] * len(arrays),
        scratch_shapes=[pltpu.SemaphoreType.DMA((sum(pieces),))],
        compiler_params=pltpu.CompilerParams(vmem_limit_bytes=4 * 2**20),
        name="place",
    )(*arrays)


def local(tokens, out_grad, expert_ids, combine, w_gate, w_up, w_down):
    results = route(tokens, out_grad, expert_ids.T, combine.T, w_gate[0], w_up[0], w_down[0])
    grad_tokens, score, gate_total, up_total, down_total = place(*results)
    return grad_tokens, score.T, gate_total[None], up_total[None], down_total[None]


def solution(mesh):
    return jax.shard_map(
        local,
        mesh=mesh,
        in_specs=(
            P("expert", "etp"),
            P("expert", "etp"),
            P("expert", None),
            P("expert", None),
            P("expert", None, "etp"),
            P("expert", None, "etp"),
            P("expert", "etp", None),
        ),
        out_specs=(
            P("expert", "etp"),
            P("expert", None),
            P("expert", None, "etp"),
            P("expert", None, "etp"),
            P("expert", "etp", None),
        ),
        check_vma=False,
    )
```

```python
import functools

import jax
import jax.numpy as jnp
from jax import lax
from jax.experimental import pallas as pl
from jax.experimental.pallas import tpu as pltpu
from jax.sharding import PartitionSpec as P

ALPHA = 1.702
MESH = pl.DeviceIdType.MESH
NX, NY, NZ, NC = 4, 4, 8, 2
CAP = 16
TOP = 4
EARLY = 128
BF16, F32 = jnp.bfloat16, jnp.float32
LAST = 2
ORDER = (
    "B0A1A2C0A3B1B2A4",
    "H0B3A5C1H1B4C2A6",
    "B5H2C3D1C4B6H3H4",
    "E1C5A7H5C6D4B7H6",
    "D5E4D6F1C7H7E5F4",
    "D3E6G1D7G4F5E3D2",
    "F6E7G5D0G6F3E2W0",
    "F7W1E0W2G3F2G7W3",
    "F0W4W5G2G0",
)
NT = (((1,), (1,)), ((), ()))
TN = (((0,), (0,)), ((), ()))


def dot(a, b, dims=(((1,), (0,)), ((), ()))):
    return lax.dot_general(a, b, dims, preferred_element_type=F32)


def route_kernel(
    dims, tok_hbm, dy_hbm, ids_ref, combine_ref, wg_hbm, wu_hbm, wd_hbm,
    out_tok, out_score, gate_buf, up_buf, down_buf,
    zbuf, zmeta, ysend, yrecv, hsend, hrecv, rows_x, rows_dy, wgu, wd, sg, gu, x_t, act_t,
    igb, own, rs1, rs2, yrs, yrr, zrs, zrr, zss, zsr, sco, sci, pmat,
    in_sem, w_sem, e_send, e_recv, z_send, z_recv, zm_send, zm_recv, y_send, y_recv, h_send, h_recv,
    x_send, x_recv, xf_send, xf_recv, r1_send, r1_recv, r2_send, r2_recv,
    yr_send, yr_recv, zr_send, zr_recv, zs_send, zs_recv, sc_send, sc_recv,
):
    tok, dl, ff, early = dims
    late = dl - early
    width = 2 * dl + 2 * (NX - 1) * early
    groups = NY * NC
    rows = groups * CAP
    e = lax.axis_index("expert")
    x = lax.axis_index("etp")
    y = e // (NZ * NC)
    z = lax.rem(e // NC, NZ)
    c = lax.rem(e, NC)
    q = y * NC + c
    xr = lax.rem(x + 1, NX)
    xl = lax.rem(x + NX - 1, NX)
    xo = lax.rem(x + 2, NX)

    def at(y_, z_, c_, x_):
        return ((y_ * NZ + z_) * NC + c_, x_)

    right, left = (e, xr), (e, xl)

    def remote(src, dst, send, recv, dev):
        return pltpu.make_async_remote_copy(
            src_ref=src, dst_ref=dst, send_sem=send, recv_sem=recv, device_id=dev, device_id_type=MESH
        )

    def lanes(start, size):
        return pl.ds(pl.multiple_of(start, 128), size)

    def group_rows(index):
        return pl.ds(pl.multiple_of(index * CAP, CAP), CAP)

    loads = [
        pltpu.make_async_copy(tok_hbm, zbuf.at[0, :, pl.ds(0, dl)], in_sem.at[0]),
        pltpu.make_async_copy(dy_hbm, zbuf.at[0, :, pl.ds(dl, dl)], in_sem.at[1]),
    ]
    weights = [
        pltpu.make_async_copy(wg_hbm, wgu.at[:, pl.ds(0, ff)], w_sem.at[0]),
        pltpu.make_async_copy(wu_hbm, wgu.at[:, pl.ds(ff, ff)], w_sem.at[1]),
        pltpu.make_async_copy(wd_hbm, wd, w_sem.at[2]),
    ]
    for cp in loads:
        cp.start()

    group_peers = [(dy, dc) for dy in range(NY) for dc in range(NC) if dy or dc]

    def group_peer(dy, dc):
        return lax.rem(y + dy, NY), lax.rem(c + dc, NC)

    barrier = pltpu.get_barrier_semaphore()
    peers = [(e, lax.rem(x + d, NX)) for d in range(1, NX)]
    peers += [at(y, lax.rem(z + d, NZ), c, x) for d in (1, NZ - 1)]
    peers += [at(group_peer(dy, dc)[0], z, group_peer(dy, dc)[1], x) for dy, dc in group_peers]
    for dev in peers:
        pl.semaphore_signal(barrier, inc=1, device_id=dev, device_id_type=MESH)
    for cp in weights:
        cp.start()

    experts = NY * NZ * NC
    ids = ids_ref[...].astype(F32)
    e_iota = lax.broadcasted_iota(jnp.int32, (experts, tok), 0).astype(F32)
    hits = [e_iota == ids[k : k + 1, :] for k in range(TOP)]
    named = functools.reduce(jnp.logical_or, hits)
    named = jnp.where(named, 1.0, 0.0).astype(BF16)
    before = lax.broadcasted_iota(jnp.int32, (tok, tok), 0) < lax.broadcasted_iota(jnp.int32, (tok, tok), 1)
    ranks = dot(named, jnp.where(before, 1.0, 0.0).astype(BF16))
    for k in range(TOP):
        rank = jnp.sum(jnp.where(hits[k], ranks, 0.0), axis=0, keepdims=True)
        zmeta[0, k : k + 1, :] = ids[k : k + 1, :] * CAP + rank
    zmeta[0, TOP : 2 * TOP, :] = combine_ref[...].astype(F32)

    def hit_masks(i):
        j = lax.broadcasted_iota(jnp.int32, (rows, tok), 0)
        expert = ((j // (CAP * NC)) * NZ + z) * NC + lax.rem(j // CAP, NC)
        code = (expert * CAP + lax.rem(j, CAP)).astype(F32)
        return [code == zmeta[i, k : k + 1, :] for k in range(TOP)]

    def own_slots(i):
        masks = hit_masks(i)
        pick = jnp.where(functools.reduce(jnp.logical_or, masks), 1.0, 0.0).astype(BF16)
        pmat[i] = pick
        scale = functools.reduce(
            jnp.add, [jnp.where(masks[k], zmeta[i, TOP + k : TOP + k + 1, :], 0.0) for k in range(TOP)]
        )
        scale = jnp.sum(scale, axis=1, keepdims=True)
        ysend[i, :, 0 : 2 * dl] = dot(pick, zbuf[i, :, 0 : 2 * dl]).astype(BF16)
        ysend[i, :, 2 * dl : 2 * dl + 128] = jnp.broadcast_to(scale, (rows, 128)).astype(BF16)

    for cp in loads:
        cp.wait()
    own_slots(0)
    pl.semaphore_wait(barrier, len(peers))

    early_copies = []
    for d in range(1, NX):
        base = 2 * dl + (NX - d - 1) * 2 * early
        for part in range(2):
            early_copies.append(remote(
                zbuf.at[0, :, pl.ds(part * dl + late, early)],
                zbuf.at[0, :, pl.ds(base + part * early, early)],
                e_send.at[d - 1, part], e_recv.at[NX - d - 1, part], (e, lax.rem(x + d, NX)),
            ))
    z_up = at(y, lax.rem(z + 1, NZ), c, x)
    z_down = at(y, lax.rem(z + NZ - 1, NZ), c, x)

    def z_own(src, dst, dev):
        part = pl.ds(0, 2 * dl)
        return (
            remote(zbuf.at[src, :, part], zbuf.at[dst, :, part], z_send.at[dst, 0], z_recv.at[dst, 0], dev),
            remote(zmeta.at[src], zmeta.at[dst], zm_send.at[dst], zm_recv.at[dst], dev),
        )

    def z_rest(src, dst, dev):
        part = pl.ds(2 * dl, width - 2 * dl)
        return (remote(zbuf.at[src, :, part], zbuf.at[dst, :, part], z_send.at[dst, 1], z_recv.at[dst, 1], dev),)


    def to_groups(src, dst, send, recv):
        for dy, dc in group_peers:
            yp, cp_ = group_peer(dy, dc)
            remote(src.at[group_rows(yp * NC + cp_)], dst.at[group_rows(q)], send, recv, at(yp, z, cp_, x)).start()
        dst[group_rows(q), :] = src[group_rows(q), :]

    def from_groups(src, dst, send, recv):
        return remote(src.at[others], dst.at[others], send, recv, right)

    to_groups(ysend.at[0], yrecv.at[0], y_send.at[0], y_recv.at[0])
    for cp in z_own(0, 1, z_up) + z_own(0, 2, z_down):
        cp.start()
    for cp in early_copies:
        cp.start()

    def onward(i):
        return at(y, lax.rem(z + 2 * lax.rem(i, 2) - 1 + NZ, NZ), c, x)

    def stage_a(i):
        for cp in z_own(0, i, z_up):
            cp.wait_recv()

        @pl.when(i + 2 < NZ - 1)
        def _():
            for cp in z_own(i, i + 2, onward(i)):
                cp.start()

        @pl.when(i == NZ - 3)
        def _():
            for cp in z_own(i, NZ - 1, z_up):
                cp.start()

        own_slots(i)
        to_groups(ysend.at[i], yrecv.at[i], y_send.at[i], y_recv.at[i])

    def stage_h(i):
        @pl.when(i == 0)
        def _():
            for cp in early_copies:
                cp.wait()
            for cp in z_rest(0, 1, z_up) + z_rest(0, 2, z_down):
                cp.start()

        @pl.when(i > 0)
        def _():
            for cp in z_rest(0, i, z_up):
                cp.wait_recv()

        @pl.when((i > 0) & (i + 2 < NZ - 1))
        def _():
            for cp in z_rest(i, i + 2, onward(i)):
                cp.start()

        @pl.when(i == NZ - 2)
        def _():
            for cp in z_rest(i, NZ - 1, z_down):
                cp.start()

        hsend[i] = dot(pmat[i], zbuf[i, :, 2 * dl : width]).astype(BF16)
        to_groups(hsend.at[i], hrecv.at[i], h_send.at[i], h_recv.at[i])

    others = pl.ds(0, rows - CAP)

    def chunk(i):
        return pl.ds(pl.multiple_of(i * rows, rows), rows)

    def x_copies(i):
        out = []
        for part, buf in enumerate((rows_x, rows_dy)):
            src = yrecv.at[i, :, pl.ds(part * dl, late)]
            dst = buf.at[chunk(i), lanes(x * dl, late)]
            out.append(remote(src, dst, x_send.at[i, part], x_recv.at[i, part], right))
            out.append(remote(src, dst, x_send.at[i, 2 + part], x_recv.at[i, 2 + part], left))
        return out

    def stage_b(i):
        from_groups(ysend.at[i], yrecv.at[i], y_send.at[i], y_recv.at[i]).wait_recv()
        to_right, to_left, dy_right, dy_left = x_copies(i)
        for cp in (to_right, dy_left, to_left, dy_right):
            cp.start()
        for part, buf in enumerate((rows_x, rows_dy)):
            buf[chunk(i), lanes(x * dl, dl)] = yrecv[i, :, part * dl : (part + 1) * dl]

    def forward_copies(i):
        tok_ref = rows_x.at[chunk(i), lanes(xl * dl, late)]
        dy_ref = rows_dy.at[chunk(i), lanes(xr * dl, late)]
        return (
            remote(tok_ref, tok_ref, xf_send.at[i, 0], xf_recv.at[i, 0], right),
            remote(dy_ref, dy_ref, xf_send.at[i, 1], xf_recv.at[i, 1], left),
        )

    def stage_c(i):
        tr, tl, dr, dl_ = x_copies(i)
        fr, fl = forward_copies(i)
        tr.wait_recv()
        fr.start()
        dl_.wait_recv()
        fl.start()

    half = rows // 2
    halves = (pl.ds(0, half), pl.ds(half, half))

    def rs1_copies(i):
        return (
            remote(igb.at[i, 2, halves[0]], rs1.at[i, 0], r1_send.at[i, 0], r1_recv.at[i, 0], right),
            remote(igb.at[i, 2, halves[1]], rs1.at[i, 1], r1_send.at[i, 1], r1_recv.at[i, 1], left),
        )

    def diagonal():
        row = lax.broadcasted_iota(jnp.int32, (rows, rows), 0)
        return row == lax.broadcasted_iota(jnp.int32, (rows, rows), 1)

    def score_copies(i):
        return [
            remote(
                sco.at[i], sci.at[i, NX - d - 1], sc_send.at[i, d - 1], sc_recv.at[i, NX - d - 1],
                (e, lax.rem(x + d, NX)),
            )
            for d in range(1, NX)
        ]

    def stage_d(i):
        tr, tl, dr, dl_ = x_copies(i)
        tl.wait_recv()
        dr.wait_recv()
        for cp in forward_copies(i):
            cp.wait_recv()
        from_groups(hsend.at[i], hrecv.at[i], h_send.at[i], h_recv.at[i]).wait_recv()
        for part, buf in enumerate((rows_x, rows_dy)):
            for d in range(1, NX):
                base = (d - 1) * 2 * early + part * early
                buf[chunk(i), lanes(lax.rem(x + d, NX) * dl + late, early)] = hrecv[i, :, base : base + early]
        rx = rows_x[chunk(i), :]
        rdy = rows_dy[chunk(i), :]
        both = dot(rx, wgu[...])
        gate_pre = both[:, 0:ff]
        up_one = both[:, ff:] + 1.0
        back = dot(rdy, wd[...], NT)
        scale = yrecv[i, :, 2 * dl : 2 * dl + 128].astype(F32)
        squash = jax.nn.sigmoid(ALPHA * gate_pre)
        glu = gate_pre * squash
        act = (glu * up_one).astype(BF16)
        act_grad = jnp.concatenate([scale] * (ff // 128), axis=1) * back
        slope = squash + ALPHA * gate_pre * squash * (1.0 - squash)
        gate_grad = (act_grad * up_one * slope).astype(BF16)
        up_grad = (act_grad * glu).astype(BF16)
        grads = jnp.concatenate([gate_grad, up_grad], axis=1)
        gu[chunk(i), :] = grads

        def piece(xd):
            return dot(grads, wgu[pl.ds(pl.multiple_of(xd * dl, 128), dl), :], NT)

        igb[i, 2] = piece(xo).astype(BF16)
        for cp in rs1_copies(i):
            cp.start()
        igb[i, 0] = piece(xr).astype(BF16)
        igb[i, 1] = piece(xl).astype(BF16)
        own[i] = piece(x)
        score = jnp.sum(act.astype(F32) * back, axis=1, keepdims=True)
        score = jnp.sum(jnp.where(diagonal(), score, 0.0), axis=0, keepdims=True)
        sco[i] = jnp.broadcast_to(score, (8, rows))
        for cp in score_copies(i):
            cp.start()
        sg[chunk(i), :] = (
            jnp.concatenate([scale] * (NX * dl // 128), axis=1) * rdy.astype(F32)
        ).astype(BF16)
        x_t[:, chunk(i)] = rx.T
        act_t[:, chunk(i)] = act.T

    def rs2_copies(i):
        return (
            remote(igb.at[i, 0], rs2.at[i, 0], r2_send.at[i, 0], r2_recv.at[i, 0], right),
            remote(igb.at[i, 1], rs2.at[i, 1], r2_send.at[i, 1], r2_recv.at[i, 1], left),
        )

    def stage_e(i):
        for side in range(2):
            rs1_copies(i)[side].wait_recv()
            igb[i, side, halves[side], :] = (
                igb[i, side, halves[side], :].astype(F32) + rs1[i, side].astype(F32)
            ).astype(BF16)
            rs2_copies(i)[side].start()

    def stage_f(i):
        for cp in rs2_copies(i):
            cp.wait_recv()
        total = own[i] + rs2[i, 0].astype(F32) + rs2[i, 1].astype(F32)
        yrs[i, :, 0:dl] = total.astype(BF16)
        for cp in score_copies(i):
            cp.wait_recv()
        score = (sco[i] + sci[i, 0] + sci[i, 1] + sci[i, 2])[0:1, :]
        score = jnp.sum(jnp.where(diagonal(), score, 0.0), axis=1, keepdims=True)
        score = jnp.broadcast_to(score, (rows, 128))
        top = score.astype(BF16).astype(F32)
        lane = lax.broadcasted_iota(jnp.int32, (rows, 128), 1)
        yrs[i, :, dl : dl + 128] = jnp.where(lane < 64, top, score - top).astype(BF16)
        to_groups(yrs.at[i], yrr.at[i], yr_send.at[i], yr_recv.at[i])

    def z_back(i):
        step = (lax.rem(i, 2) * -2 + 1) * ((i + 1) // 2)
        dev = at(y, lax.rem(z + step + NZ, NZ), c, x)
        return (
            remote(zrs.at[i], zrr.at[i], zr_send.at[i], zr_recv.at[i], dev),
            remote(zss.at[i], zsr.at[i], zs_send.at[i], zs_recv.at[i], dev),
        )

    def stage_g(i):
        from_groups(yrs.at[i], yrr.at[i], yr_send.at[i], yr_recv.at[i]).wait_recv()
        back = dot(pmat[i], yrr[i, :, 0:dl], TN)
        pair = yrr[i, :, dl : dl + 128].astype(F32)
        score = pair[:, 0:1] + pair[:, 64:65]
        masks = hit_masks(i)
        by_token = [jnp.sum(jnp.where(m, score, 0.0), axis=0, keepdims=True) for m in masks]
        by_token = jnp.concatenate(by_token + [jnp.zeros((8 - TOP, tok), F32)], axis=0)

        @pl.when(i == 0)
        def _():
            zrr[0] = back.astype(BF16)
            zsr[0] = by_token

        @pl.when(i > 0)
        def _():
            zrs[i] = back.astype(BF16)
            zss[i] = by_token
            for cp in z_back(i):
                cp.start()

        @pl.when(i > 0)
        def _():
            for cp in z_own(0, i, z_up) + z_rest(0, i, z_up):
                cp.wait_send()

        from_groups(ysend.at[i], yrecv.at[i], y_send.at[i], y_recv.at[i]).wait_send()
        from_groups(hsend.at[i], hrecv.at[i], h_send.at[i], h_recv.at[i]).wait_send()
        from_groups(yrs.at[i], yrr.at[i], yr_send.at[i], yr_recv.at[i]).wait_send()
        for cp in (*x_copies(i), *forward_copies(i), *rs1_copies(i), *rs2_copies(i), *score_copies(i)):
            cp.wait_send()

    tile = 256
    def stage_w(n):
        part = pl.ds(pl.multiple_of(n * tile, tile), tile)
        both = dot(x_t[part, :], gu[...])
        gate_buf[part, :] = both[:, 0:ff]
        up_buf[part, :] = both[:, ff:]
        down_buf[:, part] = dot(act_t[...], sg[:, part])

    for cp in weights:
        cp.wait()

    stages = dict(
        A=stage_a, B=stage_b, C=stage_c, D=stage_d, E=stage_e, F=stage_f, G=stage_g, H=stage_h, W=stage_w
    )
    names = list(stages)
    joined = "".join(ORDER)
    steps = [joined[n : n + 2] for n in range(0, len(joined), 2)]
    codes = [names.index(p[0]) * 8 + int(p[1]) for p in steps]
    words = [sum(code << (7 * k) for k, code in enumerate(codes[n : n + 4])) for n in range(0, len(codes), 4)]

    def step(s, carry):
        word = jnp.int32(words[0])
        for n in range(1, len(words)):
            word = jnp.where(s // 4 == n, jnp.int32(words[n]), word)
        code = lax.shift_right_logical(word, 7 * lax.rem(s, 4)) & 127
        for n, name in enumerate(names):
            @pl.when(code // 8 == n)
            def _():
                stages[name](lax.rem(code, 8))
        return carry

    lax.fori_loop(0, len(steps), step, 0)

    def finish(p, carry):
        i = jnp.where(p == NZ - 1, LAST, jnp.where(p < LAST, p, p + 1))
        total, score = carry
        for cp in z_back(i):
            cp.wait()
        return total + zrr[i].astype(F32), score + zsr[i]

    total, score = lax.fori_loop(1, NZ, finish, (zrr[0].astype(F32), zsr[0]))
    out_tok[...] = total.astype(BF16)
    out_score[...] = score[0:TOP, :]


def route(tokens, out_grad, ids, combine, w_gate, w_up, w_down):
    tok, dl = tokens.shape
    d, ff = w_gate.shape
    early = EARLY
    width = 2 * dl + 2 * (NX - 1) * early
    rows = NY * NC * CAP
    slots = NZ * rows
    any_spec = pl.BlockSpec(memory_space=pl.ANY)
    vmem = pl.BlockSpec(memory_space=pltpu.VMEM)
    sem = pltpu.SemaphoreType.DMA
    return pl.pallas_call(
        functools.partial(route_kernel, (tok, dl, ff, early)),
        out_shape=(
            pltpu.VMEM((tok, dl), BF16),
            pltpu.VMEM((TOP, tok), F32),
            pltpu.VMEM((d, ff), F32),
            pltpu.VMEM((d, ff), F32),
            pltpu.VMEM((ff, d), F32),
        ),
        in_specs=[any_spec, any_spec, vmem, vmem, any_spec, any_spec, any_spec],
        out_specs=(vmem, vmem, vmem, vmem, vmem),
        scratch_shapes=[
            pltpu.VMEM((NZ, tok, width), BF16),
            pltpu.VMEM((NZ, 8, tok), F32),
            pltpu.VMEM((NZ, rows, 2 * dl + 128), BF16),
            pltpu.VMEM((NZ, rows, 2 * dl + 128), BF16),
            pltpu.VMEM((NZ, rows, width - 2 * dl), BF16),
            pltpu.VMEM((NZ, rows, width - 2 * dl), BF16),
            pltpu.VMEM((slots, d), BF16),
            pltpu.VMEM((slots, d), BF16),
            pltpu.VMEM((d, 2 * ff), BF16),
            pltpu.VMEM((ff, d), BF16),
            pltpu.VMEM((slots, d), BF16),
            pltpu.VMEM((slots, 2 * ff), BF16),
            pltpu.VMEM((d, slots), BF16),
            pltpu.VMEM((ff, slots), BF16),
            pltpu.VMEM((NZ, 3, rows, dl), BF16),
            pltpu.VMEM((NZ, rows, dl), F32),
            pltpu.VMEM((NZ, 2, rows // 2, dl), BF16),
            pltpu.VMEM((NZ, 2, rows, dl), BF16),
            pltpu.VMEM((NZ, rows, dl + 128), BF16),
            pltpu.VMEM((NZ, rows, dl + 128), BF16),
            pltpu.VMEM((NZ, tok, dl), BF16),
            pltpu.VMEM((NZ, tok, dl), BF16),
            pltpu.VMEM((NZ, 8, tok), F32),
            pltpu.VMEM((NZ, 8, tok), F32),
            pltpu.VMEM((NZ, 8, rows), F32),
            pltpu.VMEM((NZ, NX - 1, 8, rows), F32),
            pltpu.VMEM((NZ, rows, tok), BF16),
            sem((2,)), sem((3,)),
            sem((NX - 1, 2)), sem((NX - 1, 2)),
            sem((NZ, 2)), sem((NZ, 2)), sem((NZ,)), sem((NZ,)),
            sem((NZ,)), sem((NZ,)), sem((NZ,)), sem((NZ,)),
            sem((NZ, 4)), sem((NZ, 4)), sem((NZ, 2)), sem((NZ, 2)),
            sem((NZ, 2)), sem((NZ, 2)), sem((NZ, 2)), sem((NZ, 2)),
            sem((NZ,)), sem((NZ,)), sem((NZ,)), sem((NZ,)), sem((NZ,)), sem((NZ,)),
            sem((NZ, NX - 1)), sem((NZ, NX - 1)),
        ],
        compiler_params=pltpu.CompilerParams(
            collective_id=0, has_side_effects=True, vmem_limit_bytes=50 * 2**20
        ),
        cost_estimate=pl.CostEstimate(
            flops=16 * slots * d * ff, bytes_accessed=12 * 2**20, transcendentals=0
        ),
        name="route",
    )(tokens, out_grad, ids, combine, w_gate, w_up, w_down)


def place_kernel(pieces, *refs):
    count = len(pieces)
    srcs, dsts, sems = refs[:count], refs[count : 2 * count], refs[2 * count]
    copies = []
    for src, dst, n in zip(srcs, dsts, pieces):
        size = src.shape[0] // n
        for k in range(n):
            part = pl.ds(k * size, size)
            copies.append(pltpu.make_async_copy(src.at[part], dst.at[part], sems.at[len(copies)]))
    for cp in copies:
        cp.start()
    for cp in copies:
        cp.wait()


def place(*arrays):
    pieces = [2 if a.size > 2**17 else 1 for a in arrays]
    return pl.pallas_call(
        functools.partial(place_kernel, pieces),
        out_shape=[jax.ShapeDtypeStruct(a.shape, a.dtype) for a in arrays],
        in_specs=[pl.BlockSpec(memory_space=pltpu.VMEM)] * len(arrays),
        out_specs=[pl.BlockSpec(memory_space=pl.ANY)] * len(arrays),
        scratch_shapes=[pltpu.SemaphoreType.DMA((sum(pieces),))],
        compiler_params=pltpu.CompilerParams(vmem_limit_bytes=4 * 2**20),
        name="place",
    )(*arrays)


def local(tokens, out_grad, expert_ids, combine, w_gate, w_up, w_down):
    results = route(tokens, out_grad, expert_ids.T, combine.T, w_gate[0], w_up[0], w_down[0])
    grad_tokens, score, gate_total, up_total, down_total = place(*results)
    return grad_tokens, score.T, gate_total[None], up_total[None], down_total[None]


def solution(mesh):
    return jax.shard_map(
        local,
        mesh=mesh,
        in_specs=(
            P("expert", "etp"),
            P("expert", "etp"),
            P("expert", None),
            P("expert", None),
            P("expert", None, "etp"),
            P("expert", None, "etp"),
            P("expert", "etp", None),
        ),
        out_specs=(
            P("expert", "etp"),
            P("expert", None),
            P("expert", None, "etp"),
            P("expert", None, "etp"),
            P("expert", "etp", None),
        ),
        check_vma=False,
    )
```
